128 devices in a mesh: dp: 8 (over y, z_hi), dap: 16 (over x, z_lo, core).
Axes of the slice: x: 4, y: 4, z: 4 (z_hi: 2, z_lo: 2; z = z_hi * 2 + z_lo), core: 2. Of those that a mesh axis runs over, the one named last changes fastest.
Arguments:
- homolog_features: bfloat16 [8, 192, 192, 64], P('dp', None, 'dap'), may hold values from -6 to 6
- edge_features: bfloat16 [8, 192, 192, 128], P('dp', 'dap'), may hold values from -6 to 6
- adjoint_edges: bfloat16 [8, 192, 192, 128], P('dp', 'dap'), may hold values from -6 to 6
- homolog_scaling_factor: float32 [64], replicated, may hold values from 0.1 to 1.9
- tensor_mapping_matrix: bfloat16 [64, 64], replicated, may hold values from -0.75 to 0.75
- tensor_final_matrix: bfloat16 [1024, 128], replicated, may hold values from -2.5 to 2.5
- tensor_final_offset: float32 [128], replicated, may hold values from -3 to 3
- edge_scaling_factor: float32 [128], replicated, may hold values from 0.1 to 1.9
- trilateral_entry_matrix: bfloat16 [128, 512], replicated, may hold values from -0.5 to 0.5
- final_sigmoid_matrix: bfloat16 [128, 128], replicated, may hold values from -0.5 to 0.5
- central_scaling_factor: float32 [128], replicated, may hold values from 0.1 to 1.9
- trilateral_final_matrix: bfloat16 [128, 128], replicated, may hold values from -0.5 to 0.5
Outputs:
- pair_out: bfloat16 [8, 192, 192, 128], P('dp', 'dap')
- pair_input_gradient: bfloat16 [8, 192, 192, 128], P('dp', 'dap')
- homolog_sensitivity: bfloat16 [8, 192, 192, 64], P('dp', None, 'dap')
- opm_gain_grad: float32 [64], replicated
- opm_proj_grad: float32 [64, 64], replicated
- opm_out_grad: float32 [1024, 128], replicated
- opm_bias_grad: float32 [128], replicated
- tri_gain_grad: float32 [128], replicated
- tri_in_grad: float32 [128, 512], replicated
- tri_gate_grad: float32 [128, 128], replicated
- mid_gain_grad: float32 [128], replicated
- tri_out_grad: float32 [128, 128], replicated
The draws below stay inside these ranges and needn't reach their ends.
All inputs are finite; a program needn't handle non-finite values.
Results may differ from the reference program's by a relative error of at most 0.025.
Values may be sent and summed in bfloat16 or wider, within the bound.
No kernel may reach another device: no remote copies, remote signals or barrier semaphores. Data moves between devices by JAX's collectives and lax.ppermute only.
A program may use at most 192 MiB of HBM per device.

```python
import jax
import jax.numpy as jnp
from jax import lax

HOMOLOG_FEATURES = 64
CZ = 128
HIDDEN_FEATURES = 32
TRI_HID = 128
TILE_AMINO_ACIDS = 192
TILE_HOMOLOGS = 192
TILE_TOTAL = 8


def block_scale(rng, dims, cuts, smallest, high):
    def one(dim, shards_of):
        heights = jax.random.uniform(jax.random.fold_in(jax.random.fold_in(rng, 6), dim), (shards_of,), jnp.float32, smallest / len(cuts), high / len(cuts))
        return jnp.repeat(jnp.exp(heights), dims[dim] // shards_of).reshape((-1,) + (1,) * (len(dims) - dim - 1))

    factor_of = one(*cuts[0])
    for cut in cuts[1:]:
        factor_of = factor_of * one(*cut)
    return factor_of


def noise(rng, dims, scale, bound, pieces=(), held_as=jnp.bfloat16):
    loudness = block_scale(rng, dims, pieces, -0.22, 0.18) if pieces else 1.0
    entries = jax.random.normal(rng, dims, jnp.float32) * scale * loudness
    return jnp.minimum(jnp.maximum(entries, -bound), bound).astype(held_as)


def setup_inputs(seed: int = 0) -> dict:
    key_of = jax.random.split(jax.random.key(seed), 13)
    homolog_features = noise(key_of[0], (TILE_TOTAL, TILE_HOMOLOGS, TILE_AMINO_ACIDS, HOMOLOG_FEATURES), 1.0, 6.0, ((0, 8), (2, 16)))
    edge_features = noise(key_of[1], (TILE_TOTAL, TILE_AMINO_ACIDS, TILE_AMINO_ACIDS, CZ), 1.0, 6.0, ((0, 8), (1, 16)))
    adjoint_edges = noise(key_of[2], (TILE_TOTAL, TILE_AMINO_ACIDS, TILE_AMINO_ACIDS, CZ), 1.0, 6.0, ((0, 8), (1, 16)))
    homolog_scaling_factor = jnp.clip(1.0 + 0.18 * jax.random.normal(key_of[3], (HOMOLOG_FEATURES,), jnp.float32), 0.1, 1.9)
    tensor_mapping_matrix = noise(key_of[4], (HOMOLOG_FEATURES, 2 * HIDDEN_FEATURES), HOMOLOG_FEATURES ** -0.5, 0.75)
    tensor_final_matrix = noise(key_of[5], (HIDDEN_FEATURES * HIDDEN_FEATURES, CZ), (max(1, HIDDEN_FEATURES * HIDDEN_FEATURES // TILE_HOMOLOGS)) ** -0.5, 2.5)
    tensor_final_offset = noise(key_of[6], (CZ,), 0.5, 3.0, (), jnp.float32)
    edge_scaling_factor = jnp.clip(1.0 + 0.18 * jax.random.normal(key_of[7], (CZ,), jnp.float32), 0.1, 1.9)
    trilateral_entry_matrix = noise(key_of[8], (CZ, 4 * TRI_HID), CZ ** -0.5, 0.5)
    final_sigmoid_matrix = noise(key_of[9], (CZ, CZ), CZ ** -0.5, 0.5)
    central_scaling_factor = jnp.clip(1.0 + 0.18 * jax.random.normal(key_of[10], (TRI_HID,), jnp.float32), 0.1, 1.9)
    trilateral_final_matrix = noise(key_of[11], (TRI_HID, CZ), TRI_HID ** -0.5, 0.5)
    return {"homolog_features": homolog_features, "edge_features": edge_features, "adjoint_edges": adjoint_edges, "homolog_scaling_factor": homolog_scaling_factor, "tensor_mapping_matrix": tensor_mapping_matrix, "tensor_final_matrix": tensor_final_matrix, "tensor_final_offset": tensor_final_offset, "edge_scaling_factor": edge_scaling_factor, "trilateral_entry_matrix": trilateral_entry_matrix, "final_sigmoid_matrix": final_sigmoid_matrix, "central_scaling_factor": central_scaling_factor, "trilateral_final_matrix": trilateral_final_matrix}


EPSILON = 1e-05

def layer_norm_forward(values):
    centred = values - lax.optimization_barrier(jnp.mean(values, -1, keepdims=True))
    inverse = lax.rsqrt(lax.optimization_barrier(jnp.mean(centred * centred, -1, keepdims=True)) + EPSILON)
    return (centred * inverse, inverse)

def standardize_adjoint(grad_hat, normed, inverse):
    first = lax.optimization_barrier(jnp.mean(grad_hat, -1, keepdims=True))
    second = lax.optimization_barrier(jnp.mean(grad_hat * normed, -1, keepdims=True))
    return (grad_hat - first - normed * second) * inverse

def trilateral_contraction(form, left, right):
    return jnp.einsum(form, left.astype(jnp.float32), right.astype(jnp.float32))

def tile_iteration_routine(tile_number, parameter_collection):
    homolog_lines, pair_row_block, cotangent_row_block = tile_number
    homolog_scaling_factor, tensor_mapping_matrix, tensor_final_matrix, tensor_final_offset, edge_scaling_factor, trilateral_entry_matrix, final_sigmoid_matrix, central_scaling_factor, trilateral_final_matrix = parameter_collection
    opm_half = tensor_mapping_matrix.shape[1] // 2
    width = trilateral_final_matrix.shape[0]
    sequence_depth = homolog_lines.shape[0]
    length = pair_row_block.shape[0]
    homolog_standardized, homolog_reciprocal_spread = layer_norm_forward(homolog_lines.astype(jnp.float32))
    alignment_normalized = (homolog_standardized * homolog_scaling_factor).astype(jnp.bfloat16)
    projected_pairs = trilateral_contraction('zft,tr->zfr', alignment_normalized, tensor_mapping_matrix).astype(jnp.bfloat16)
    left_projection_rows = projected_pairs[..., :opm_half]
    right_projection_rows = projected_pairs[..., opm_half:]
    outer_product_block = (trilateral_contraction('xeb,xdc->edbc', left_projection_rows, right_projection_rows) / sequence_depth).astype(jnp.bfloat16)
    outer_product_block = outer_product_block.reshape(length, length, opm_half * opm_half)
    pair_mid = pair_row_block.astype(jnp.float32) + (trilateral_contraction('ijf,fd->ijd', outer_product_block, tensor_final_matrix) + tensor_final_offset)
    pair_hat, pair_inv = layer_norm_forward(pair_mid)
    pair_normed = (pair_hat * edge_scaling_factor).astype(jnp.bfloat16)
    raw = trilateral_contraction('kid,de->kie', pair_normed, trilateral_entry_matrix)
    left_sig = jax.nn.sigmoid(raw[..., :width])
    right_sig = jax.nn.sigmoid(raw[..., 2 * width:3 * width])
    left_value = raw[..., width:2 * width]
    right_value = raw[..., 3 * width:]
    left_edge = (left_sig * left_value).astype(jnp.bfloat16)
    right_edge = (right_sig * right_value).astype(jnp.bfloat16)
    mixed = trilateral_contraction('kic,kjc->ijc', left_edge, right_edge)
    mixed_hat, mixed_inv = layer_norm_forward(mixed)
    mixed_normed = (mixed_hat * central_scaling_factor).astype(jnp.bfloat16)
    gate = jax.nn.sigmoid(trilateral_contraction('ijd,de->ije', pair_normed, final_sigmoid_matrix))
    update = trilateral_contraction('ijc,cd->ijd', mixed_normed, trilateral_final_matrix)
    pair_new = pair_mid + gate * update
    pair_result_state = pair_new.astype(jnp.bfloat16)
    upstream = cotangent_row_block.astype(jnp.float32)
    grad_update = (upstream * gate).astype(jnp.bfloat16)
    grad_gate = (upstream * update * gate * (1.0 - gate)).astype(jnp.bfloat16)
    triangle_output_gradient = trilateral_contraction('ijc,ijd->cd', mixed_normed, grad_update)
    triangle_gate_gradient = trilateral_contraction('ijc,ijd->cd', pair_normed, grad_gate)
    grad_mixed_normed = trilateral_contraction('ijd,cd->ijc', grad_update, trilateral_final_matrix)
    middle_gain_gradient = lax.optimization_barrier(jnp.sum(grad_mixed_normed * mixed_hat, (0, 1)))
    grad_mixed = standardize_adjoint(grad_mixed_normed * central_scaling_factor, mixed_hat, mixed_inv).astype(jnp.bfloat16)
    grad_left = trilateral_contraction('ijc,kjc->kic', grad_mixed, right_edge)
    grad_right = trilateral_contraction('ijc,kic->kjc', grad_mixed, left_edge)
    grad_raw = jnp.concatenate([grad_left * left_value * left_sig * (1.0 - left_sig), grad_left * left_sig, grad_right * right_value * right_sig * (1.0 - right_sig), grad_right * right_sig], -1).astype(jnp.bfloat16)
    triangle_input_gradient = trilateral_contraction('kid,kie->de', pair_normed, grad_raw)
    grad_normed = trilateral_contraction('kie,de->kid', grad_raw, trilateral_entry_matrix) + trilateral_contraction('kie,de->kid', grad_gate, final_sigmoid_matrix)
    triangle_gain_gradient = lax.optimization_barrier(jnp.sum(grad_normed * pair_hat, (0, 1)))
    grad_mid = upstream + standardize_adjoint(grad_normed * edge_scaling_factor, pair_hat, pair_inv)
    pair_input_gradient = grad_mid.astype(jnp.bfloat16)
    output_bias_gradient = lax.optimization_barrier(jnp.sum(grad_mid, (0, 1)))
    outer_output_gradient = trilateral_contraction('ijf,ijd->fd', outer_product_block, pair_input_gradient)
    outer_product_gradient = trilateral_contraction('ijd,fd->ijf', pair_input_gradient, tensor_final_matrix).astype(jnp.bfloat16)
    outer_product_gradient = outer_product_gradient.reshape(length, length, opm_half, opm_half)
    left_projection_gradient = trilateral_contraction('yxet,vxt->vye', outer_product_gradient, right_projection_rows) / sequence_depth
    right_projection_gradient = trilateral_contraction('ynmv,oym->onv', outer_product_gradient, left_projection_rows) / sequence_depth
    mapping_sensitivity = jnp.concatenate([left_projection_gradient, right_projection_gradient], -1).astype(jnp.bfloat16)
    outer_projection_gradient = trilateral_contraction('keb,kex->bx', alignment_normalized, mapping_sensitivity)
    standardized_homolog_adjoint = trilateral_contraction('dvk,gk->dvg', mapping_sensitivity, tensor_mapping_matrix)
    tensor_scaling_sensitivity = lax.optimization_barrier(jnp.sum(standardized_homolog_adjoint * homolog_standardized, (0, 1)))
    homolog_sensitivity = standardize_adjoint(standardized_homolog_adjoint * homolog_scaling_factor, homolog_standardized, homolog_reciprocal_spread).astype(jnp.bfloat16)
    return (pair_result_state, pair_input_gradient, homolog_sensitivity, tensor_scaling_sensitivity, outer_projection_gradient, outer_output_gradient, output_bias_gradient, triangle_gain_gradient, triangle_input_gradient, triangle_gate_gradient, middle_gain_gradient, triangle_output_gradient)

def reference(homolog_features, edge_features, adjoint_edges, homolog_scaling_factor, tensor_mapping_matrix, tensor_final_matrix, tensor_final_offset, edge_scaling_factor, trilateral_entry_matrix, final_sigmoid_matrix, central_scaling_factor, trilateral_final_matrix):
    parameter_collection = (homolog_scaling_factor, tensor_mapping_matrix, tensor_final_matrix, tensor_final_offset, edge_scaling_factor, trilateral_entry_matrix, final_sigmoid_matrix, central_scaling_factor, trilateral_final_matrix)
    tile_returns = lax.map(lambda tile_number: tile_iteration_routine(tile_number, parameter_collection), (homolog_features, edge_features, adjoint_edges))
    factor = 1.0 / (TILE_TOTAL * TILE_AMINO_ACIDS)
    grads = [lax.optimization_barrier(jnp.sum(item, 0)) * factor for item in tile_returns[3:]]
    return (tile_returns[0], tile_returns[1], tile_returns[2], grads[0], grads[1], grads[2], grads[3], grads[4], grads[5], grads[6], grads[7], grads[8])
```

```python
import jax
import jax.numpy as jnp
from jax import lax
from jax.experimental import pallas as pl
from jax.experimental.pallas import tpu as pltpu
from jax.sharding import PartitionSpec as P

EPSILON = 1e-05
BF = jnp.bfloat16
F32 = jnp.float32
WIDE = 256


def nn(a, b):
    return lax.dot_general(a, b, (((1,), (0,)), ((), ())), preferred_element_type=F32)


def nt(a, b):
    return lax.dot_general(a, b, (((1,), (1,)), ((), ())), preferred_element_type=F32)


def tn(a, b):
    return lax.dot_general(a, b, (((0,), (0,)), ((), ())), preferred_element_type=F32)


def norm(v):
    centred = v - jnp.mean(v, 0, keepdims=True)
    inverse = lax.rsqrt(jnp.mean(centred * centred, 0, keepdims=True) + EPSILON)
    return centred * inverse, inverse


def norm_back(h, hat, inverse):
    first = jnp.mean(h, 0, keepdims=True)
    second = jnp.mean(h * hat, 0, keepdims=True)
    return (h - first - hat * second) * inverse


def sigmoid(v):
    return 1.0 / (1.0 + jnp.exp(-v))


def pad_rows(v, rows):
    return jnp.concatenate([v, jnp.zeros((rows - v.shape[0],) + v.shape[1:], v.dtype)], 0)


def flip(v):
    return pad_rows(v, WIDE).T


def low_half(v):
    lane = lax.broadcasted_iota(jnp.int32, v.shape, v.ndim - 1)
    return jnp.where(lane < 64, v, 0.0)


def pack(a, b):
    tail = low_half(a[:, 128:]) + pltpu.roll(low_half(b[:, 128:]), 64, 1)
    return a[:, :128], b[:, :128], tail


def unpack(t0, t1, t2):
    return (t0, low_half(t2)), (t1, low_half(pltpu.roll(t2, 64, 1)))


def call(kernel, outs, scratch, *operands, smem=0):
    specs = [pl.BlockSpec(memory_space=pltpu.SMEM)] * smem
    specs += [pl.BlockSpec(memory_space=pltpu.VMEM)] * (len(operands) - smem)
    return pl.pallas_call(
        kernel,
        out_shape=[jax.ShapeDtypeStruct(s, t) for s, t in outs],
        in_specs=specs,
        out_specs=[pl.BlockSpec(memory_space=pltpu.VMEM)] * len(outs),
        scratch_shapes=[pltpu.VMEM(s, t) for s, t in scratch],
        compiler_params=pltpu.CompilerParams(vmem_limit_bytes=50 * 1024 * 1024),
    )(*operands)


def project_kernel(x_ref, gain_ref, wt_ref, left_ref, lsend_ref, rsend_ref):
    pairs = x_ref.shape[0]
    width = wt_ref.shape[1]
    half = wt_ref.shape[0] // 2

    @pl.loop(0, pairs)
    def _(m):
        x = flip(x_ref[m].astype(F32))
        both = []
        for o in range(2):
            hat, _ = norm(x[o * width : (o + 1) * width])
            normed = (hat * gain_ref[...]).astype(BF)
            proj = nn(wt_ref[...], normed)
            both.append(proj)
            left_ref[2 * m + o] = proj[:half].astype(BF)
        for t, v in enumerate(pack(both[0][:half], both[1][:half])):
            lsend_ref[m, t] = v.astype(BF)
        for t, v in enumerate(pack(both[0][half:], both[1][half:])):
            rsend_ref[m, t] = v.astype(BF)


def outer_kernel(
    par_ref, own_ref, other_ref, left_ref, edge_ref, wt_ref, bias_ref, gain_ref, entry_ref,
    send_ref, mid_ref, normed_ref, right_ref, outer_ref, head, tail,
):
    chips, pairs, _, half, _ = own_ref.shape
    rows = left_ref.shape[0]
    length = edge_ref.shape[1]
    depth = 1.0 / length
    par = par_ref[0]
    for source, p in ((own_ref, par), (other_ref, 1 - par)):

        @pl.loop(0, chips)
        def _(chip):
            for m in range(pairs):
                t = source[chip, m].astype(F32)
                base = pl.multiple_of(((2 * chip + p) * rows + 2 * m) * half, half)
                for o, (a, b) in enumerate(unpack(t[0], t[1], t[2])):
                    head[pl.ds(base + o * half, half), :] = a
                    tail[pl.ds(base + o * half, half), :] = b

    left = left_ref[...].reshape(rows * half, WIDE)

    @pl.loop(0, half)
    def _(q):
        a = head[pl.ds(q, length, stride=half), :]
        b = tail[pl.ds(q, length, stride=half), :]
        r = pad_rows(jnp.concatenate([a, b], 1), WIDE).astype(BF)
        right_ref[q] = r
        o = (nt(left, r) * depth).astype(BF)
        at = pl.ds(pl.multiple_of(q * half, half), half)
        for i in range(rows):
            outer_ref[i, at, :] = o[i * half : (i + 1) * half]

    devices, _, _, sixteen, _ = send_ref.shape

    @pl.loop(0, pairs)
    def _(m):
        both = []
        for o in range(2):
            i = 2 * m + o
            mid = flip(edge_ref[i].astype(F32)) + (nn(wt_ref[...], outer_ref[i]) + bias_ref[...])
            mid_ref[i] = mid
            hat, _ = norm(mid)
            normed = (hat * gain_ref[...]).astype(BF)
            normed_ref[i] = normed
            raw = nn(entry_ref[...], normed)
            cut = raw.shape[0] // 2
            both.append(sigmoid(raw[:cut]) * raw[cut:])
        for t, v in enumerate(pack(*both)):
            send_ref[:, m, t] = v.reshape(devices, sixteen, 128).astype(BF)


def load_wide(head, tail, start, count, stride):
    a = head[pl.ds(start, count, stride=stride), :]
    b = tail[pl.ds(start, count, stride=stride), :]
    return jnp.concatenate([a, b], 1)


def store_wide(head, tail, start, count, stride, v):
    head[pl.ds(start, count, stride=stride), :] = v[:, :128]
    tail[pl.ds(start, count, stride=stride), :] = v[:, 128:]


def spread(source, head, tail):
    devices, pairs, _, high, _ = source.shape

    @pl.loop(0, devices)
    def _(d):
        for m in range(pairs):
            t = source[d, m].astype(F32)
            base = pl.multiple_of((d * pairs + m) * 2 * high, 2 * high)
            for o, (a, b) in enumerate(unpack(t[0], t[1], t[2])):
                head[pl.ds(base + o * high, high), :] = a
                tail[pl.ds(base + o * high, high), :] = b


def gather_up(head, tail, target):
    devices, pairs, _, high, _ = target.shape

    @pl.loop(0, devices)
    def _(d):
        for m in range(pairs):
            base = pl.multiple_of((d * pairs + m) * 2 * high, 2 * high)
            wide = [
                jnp.concatenate(
                    [head[pl.ds(base + o * high, high), :], tail[pl.ds(base + o * high, high), :]], 1
                )
                for o in range(2)
            ]
            for t, v in enumerate(pack(*wide)):
                target[d, m, t] = v.astype(BF)


def triangle_kernel(edges_ref, send_ref, left_ref, right_ref, head, tail, mhead, mtail):
    channels, length, _ = left_ref.shape
    spread(edges_ref, head, tail)
    for c in range(channels):
        a = load_wide(head, tail, c, length, 2 * channels).astype(BF)
        b = load_wide(head, tail, channels + c, length, 2 * channels).astype(BF)
        left_ref[c] = a
        right_ref[c] = b
        mixed = tn(a, b)[:length]
        store_wide(mhead, mtail, c, length, channels, mixed)
    gather_up(mhead, mtail, send_ref)


def triangle_back_kernel(grads_ref, left_ref, right_ref, send_ref, head, tail, mhead, mtail):
    channels, length, _ = left_ref.shape
    spread(grads_ref, mhead, mtail)
    for c in range(channels):
        g = pad_rows(load_wide(mhead, mtail, c, length, channels), WIDE).astype(BF)
        store_wide(head, tail, c, length, 2 * channels, nt(right_ref[c], g))
        store_wide(head, tail, channels + c, length, 2 * channels, nn(left_ref[c], g))
    gather_up(head, tail, send_ref)


def update_kernel(
    mixed_ref, mid_ref, normed_ref, adj_ref, cgain_ref, wf_ref, wft_ref, wgt_ref,
    out_ref, send_ref, ggate_ref, wfg_ref, wgg_ref, msum_ref, acc,
):
    devices, quads, _, sixteen, _ = mixed_ref.shape
    length = out_ref.shape[1]
    channels = wf_ref.shape[0]
    eight = channels // devices
    wfg_ref[...] = jnp.zeros_like(wfg_ref)
    wgg_ref[...] = jnp.zeros_like(wgg_ref)
    acc[...] = jnp.zeros_like(acc)

    @pl.loop(0, quads)
    def _(n):
        t = [mixed_ref[:, n, k].astype(F32).reshape(devices * sixteen, 128) for k in range(3)]
        packed = []
        for mo, (a, b) in enumerate(unpack(*t)):
            block = jnp.concatenate([a, b], 1).reshape(devices, 2, eight, WIDE)
            grads = []
            for o in range(2):
                i = 4 * n + 2 * mo + o
                mixed = block[:, o].reshape(channels, WIDE)
                hat, inverse = norm(mixed)
                mn = (hat * cgain_ref[...]).astype(BF)
                normed = normed_ref[i]
                gate = sigmoid(nn(wgt_ref[...], normed))
                update = nn(wft_ref[...], mn)
                new = mid_ref[i] + gate * update
                out_ref[i] = new.T[:length].astype(BF)
                up = flip(adj_ref[i].astype(F32))
                gu = (up * gate).astype(BF)
                gg = (up * update * gate * (1.0 - gate)).astype(BF)
                ggate_ref[i] = gg
                wfg_ref[...] += nt(mn, gu)
                wgg_ref[...] += nt(normed, gg)
                gmn = nn(wf_ref[...], gu)
                acc[...] += gmn * hat
                grads.append(
                    norm_back(gmn * cgain_ref[...], hat, inverse).reshape(devices, 1, eight, WIDE)
                )
            packed.append(jnp.concatenate(grads, 1).reshape(devices * sixteen, WIDE))
        for k, v in enumerate(pack(*packed)):
            send_ref[:, n, k] = v.reshape(devices, sixteen, 128).astype(BF)

    msum_ref[...] = jnp.sum(acc[...].T, 0, keepdims=True)


def edge_back_kernel(
    grads_ref, mid_ref, normed_ref, ggate_ref, adj_ref, gain_ref, entryt_ref, entry_ref, wg_ref,
    pgrad_ref, pgradt_ref, send_ref, win_ref, gsum_ref, bsum_ref, gacc, bacc, rows,
):
    devices, pairs, _, sixteen, _ = grads_ref.shape
    count, length, channels = pgrad_ref.shape
    win_ref[...] = jnp.zeros_like(win_ref)
    gacc[...] = jnp.zeros_like(gacc)
    bacc[...] = jnp.zeros_like(bacc)

    @pl.loop(0, pairs)
    def _(m):
        t = [grads_ref[:, m, k].astype(F32).reshape(devices * sixteen, 128) for k in range(3)]
        for o, (a, b) in enumerate(unpack(*t)):
            i = 2 * m + o
            grad = jnp.concatenate([a, b], 1)
            normed = normed_ref[i]
            raw = nn(entryt_ref[...], normed)
            cut = raw.shape[0] // 2
            sig = sigmoid(raw[:cut])
            gs = grad * sig
            graw = jnp.concatenate([gs * raw[cut:] * (1.0 - sig), gs], 0).astype(BF)
            win_ref[...] += nt(graw, normed)
            gpn = nn(entry_ref[...], graw) + nn(wg_ref[...], ggate_ref[i])
            hat, inverse = norm(mid_ref[i])
            gacc[...] += gpn * hat
            up = flip(adj_ref[i].astype(F32))
            gmid = up + norm_back(gpn * gain_ref[...], hat, inverse)
            bacc[...] += gmid
            pgradt_ref[i] = gmid.astype(BF)
            turned = gmid.T[:length]
            pgrad_ref[i] = turned.astype(BF)
            rows[pl.ds(i, length, stride=count), :] = turned

    send_ref[...] = rows[...].astype(BF)
    gsum_ref[...] = jnp.sum(gacc[...].T, 0, keepdims=True)
    bsum_ref[...] = jnp.sum(bacc[...].T, 0, keepdims=True)


def outer_back_kernel(
    pgradt_ref, right_ref, outer_ref, w_ref, grad_ref, wout_ref, stage,
):
    count, _, _ = pgradt_ref.shape
    half = right_ref.shape[0]
    length = 1.0 / 192
    group = stage.shape[2] // WIDE

    @pl.loop(0, count)
    def _(i):
        g = nn(w_ref[...], pgradt_ref[i]).astype(BF)
        at = pl.ds(pl.multiple_of(i * half, half), half)
        for q in range(half):
            stage[q // group, at, (q % group) * WIDE : (q % group + 1) * WIDE] = g[
                q * half : (q + 1) * half
            ]

    grad_ref[...] = jnp.zeros_like(grad_ref)

    @pl.loop(0, half // group)
    def _(k):
        r = right_ref[pl.ds(k * group, group)].reshape(group * WIDE, WIDE)
        grad_ref[...] += nn(stage[k], r)

    grad_ref[...] = grad_ref[...] * length
    wout_ref[...] = jnp.zeros_like(wout_ref)

    @pl.loop(0, count // 2)
    def _(m):
        a = jnp.concatenate([outer_ref[2 * m], outer_ref[2 * m + 1]], 1)
        b = jnp.concatenate([pgradt_ref[2 * m], pgradt_ref[2 * m + 1]], 1)
        wout_ref[...] += nt(a, b)


def column_kernel(
    pcol_ref, lgath_ref, w_ref, gleft_ref, x_ref, mgain_ref, wmap_ref,
    out_ref, wproj_ref, msum_ref, prow, head, tail, stage, lefts, gright, macc,
):
    devices, many, channels = pcol_ref.shape
    _, pairs, _, half, _ = lgath_ref.shape
    count = 2 * pairs
    length = devices * count
    group = stage.shape[2] // WIDE

    @pl.loop(0, devices)
    def _(d):
        prow[pl.ds(pl.multiple_of(d * many, 8), many), :] = pcol_ref[d].astype(F32)
        for m in range(pairs):
            t = lgath_ref[d, m].astype(F32)
            for o, (a, b) in enumerate(unpack(t[0], t[1], t[2])):
                base = pl.multiple_of(((2 * m + o) * devices + d) * half, half)
                head[pl.ds(base, half), :] = a
                tail[pl.ds(base, half), :] = b

    @pl.loop(0, count)
    def _(j):
        p = jnp.concatenate(
            [prow[pl.ds(j * count + i, devices, stride=many), :] for i in range(count)], 0
        )
        g = nt(w_ref[...], pad_rows(p, WIDE).astype(BF)).astype(BF)
        at = pl.ds(pl.multiple_of(j * half, half), half)
        for q in range(half):
            stage[q // group, at, (q % group) * WIDE : (q % group + 1) * WIDE] = g[
                q * half : (q + 1) * half
            ]

    @pl.loop(0, half)
    def _(q):
        lefts[q] = pad_rows(load_wide(head, tail, q, length, half), WIDE).astype(BF)

    gright[...] = jnp.zeros_like(gright)

    @pl.loop(0, half // group)
    def _(k):
        r = lefts[pl.ds(k * group, group)].reshape(group * WIDE, WIDE)
        gright[...] += nn(stage[k], r)

    width = wmap_ref.shape[0]
    wproj_ref[...] = jnp.zeros_like(wproj_ref)
    macc[...] = jnp.zeros_like(macc)

    @pl.loop(0, pairs)
    def _(m):
        x = flip(x_ref[m].astype(F32))
        both = []
        for o in range(2):
            hat, inverse = norm(x[o * width : (o + 1) * width])
            normed = (hat * mgain_ref[...]).astype(BF)
            at = pl.ds(pl.multiple_of((2 * m + o) * half, half), half)
            g = jnp.concatenate([gleft_ref[at, :], gright[at, :] * (1.0 / length)], 0).astype(BF)
            wproj_ref[...] += nt(normed, g)
            gn = nn(wmap_ref[...], g)
            macc[...] += gn * hat
            both.append(norm_back(gn * mgain_ref[...], hat, inverse))
        out_ref[m] = jnp.concatenate(both, 0).T[:length].astype(BF)

    total = macc[...]
    msum_ref[...] = jnp.sum(jnp.concatenate([total, jnp.zeros_like(total)], 0).T, 0, keepdims=True)


def exchange(v, axes="dap", groups=None):
    return lax.all_to_all(
        v, axes, split_axis=0, concat_axis=0, tiled=True, axis_index_groups=groups
    )


def local(
    homolog_features,
    edge_features,
    adjoint_edges,
    homolog_scaling_factor,
    tensor_mapping_matrix,
    tensor_final_matrix,
    tensor_final_offset,
    edge_scaling_factor,
    trilateral_entry_matrix,
    final_sigmoid_matrix,
    central_scaling_factor,
    trilateral_final_matrix,
):
    n = lax.axis_size("dap")
    everyone = n * lax.axis_size("dp")
    msa = homolog_features[0]
    depth, count, width = msa.shape
    length = edge_features.shape[2]
    pairs = count // 2
    half = tensor_mapping_matrix.shape[1] // 2
    channels = edge_features.shape[3]
    eight = channels // n
    edges = edge_features[0]
    adjoint = adjoint_edges[0]
    column = lambda v: v.reshape(-1, 1)

    x = msa.reshape(depth, pairs, 2 * width).transpose(1, 0, 2)
    left, left_send, right_send = call(
        project_kernel,
        [((count, half, WIDE), BF), ((pairs, 3, half, 128), BF), ((pairs, 3, half, 128), BF)],
        [],
        x, column(homolog_scaling_factor), tensor_mapping_matrix.T,
    )
    chips = n // 2
    groups = [list(range(0, n, 2)), list(range(1, n, 2))]
    own = exchange(
        jnp.broadcast_to(right_send, (chips,) + right_send.shape), groups=groups
    )
    other = lax.ppermute(own, "dap", [(i, i ^ 1) for i in range(n)])
    left_all = lax.all_gather(left_send, "dap", axis=0, tiled=False)
    parity = lax.rem(lax.axis_index("dap"), 2).astype(jnp.int32).reshape(1)

    qp = tensor_final_matrix.reshape(half, half, channels).transpose(1, 0, 2)
    qp = qp.reshape(half * half, channels)
    entry = trilateral_entry_matrix.reshape(channels, 2, 2, n, eight).transpose(0, 2, 3, 1, 4)
    entry = entry.reshape(channels, 4 * channels)
    edge_send, mid, normed, right, outer = call(
        outer_kernel,
        [
            ((n, pairs, 3, 2 * eight, 128), BF),
            ((count, channels, WIDE), F32),
            ((count, channels, WIDE), BF),
            ((half, WIDE, WIDE), BF),
            ((count, half * half, WIDE), BF),
        ],
        [((length * half, 128), F32)] * 2,
        parity, own, other, left, edges, qp.T, column(tensor_final_offset),
        column(edge_scaling_factor), entry.T, smem=1,
    )
    edge_cols = exchange(edge_send)
    mixed_send, left_cols, right_cols = call(
        triangle_kernel,
        [
            ((n, pairs // 2, 3, 2 * eight, 128), BF),
            ((eight, length, WIDE), BF),
            ((eight, length, WIDE), BF),
        ],
        [((length * 2 * eight, 128), F32)] * 2 + [((length * eight, 128), F32)] * 2,
        edge_cols,
    )
    mixed = exchange(mixed_send)
    square = ((channels, channels), F32)
    row = ((1, channels), F32)
    pair_out, grad_send, grad_gate, tri_out, tri_gate, mid_gain = call(
        update_kernel,
        [
            (edges.shape, BF),
            ((n, pairs // 2, 3, 2 * eight, 128), BF),
            ((count, channels, WIDE), BF),
            square, square, row,
        ],
        [((channels, WIDE), F32)],
        mixed, mid, normed, adjoint, column(central_scaling_factor),
        trilateral_final_matrix, trilateral_final_matrix.T, final_sigmoid_matrix.T,
    )
    grad_cols = exchange(grad_send)
    (back_send,) = call(
        triangle_back_kernel,
        [((n, pairs, 3, 2 * eight, 128), BF)],
        [((length * 2 * eight, 128), F32)] * 2 + [((length * eight, 128), F32)] * 2,
        grad_cols, left_cols, right_cols,
    )
    back = exchange(back_send)
    pgrad, pgradt, pgrad_send, tri_in, tri_gain, bias = call(
        edge_back_kernel,
        [
            (edges.shape, BF),
            ((count, channels, WIDE), BF),
            ((length * count, channels), BF),
            ((4 * channels, channels), F32),
            row, row,
        ],
        [((channels, WIDE), F32)] * 2 + [((length * count, channels), F32)],
        back, mid, normed, grad_gate, adjoint, column(edge_scaling_factor),
        entry.T, entry, final_sigmoid_matrix,
    )
    pgrad_cols = exchange(pgrad_send.reshape(n, count * count, channels))
    group = 4
    stage = ((half // group, count * half, group * WIDE), BF)
    grad_left, opm_out = call(
        outer_back_kernel,
        [((count * half, WIDE), F32), ((half * half, channels), F32)],
        [stage],
        pgradt, right, outer, qp,
    )
    sens, opm_proj, opm_gain = call(
        column_kernel,
        [((pairs, length, 2 * width), BF), ((width, 2 * half), F32), ((1, 2 * width), F32)],
        [
            ((length * count, channels), F32),
            ((length * half, 128), F32),
            ((length * half, 128), F32),
            stage,
            ((half, WIDE, WIDE), BF),
            ((count * half, WIDE), F32),
            ((width, WIDE), F32),
        ],
        pgrad_cols, left_all, tensor_final_matrix, grad_left, x,
        column(homolog_scaling_factor), tensor_mapping_matrix,
    )
    sensitivity = sens.transpose(1, 0, 2).reshape(depth, count, width)

    factor = 1.0 / (lax.axis_size("dp") * length)
    parts = [opm_out, tri_in, tri_gate, tri_out, opm_proj.reshape(-1, 128)]
    parts += [mid_gain, tri_gain, bias, opm_gain]
    used = sum(p.shape[0] for p in parts)
    each = -(-used // (16 * everyone)) * 16
    parts.append(jnp.zeros((each * everyone - used, 128), F32))
    mine = exchange(
        jnp.concatenate(parts, 0).astype(BF).reshape(everyone, each, 128), ("dp", "dap")
    )
    mine = (jnp.sum(mine.astype(F32), 0) * factor).astype(BF)
    total = exchange(jnp.broadcast_to(mine, (everyone, each, 128)), ("dp", "dap"))
    total = total.reshape(everyone * each, 128).astype(F32)
    found = []
    at = 0
    for p in parts[:-1]:
        found.append(total[at : at + p.shape[0]])
        at += p.shape[0]
    opm_out, tri_in, tri_gate, tri_out, opm_proj, mid_gain, tri_gain, bias, opm_gain = found
    opm_out = opm_out.reshape(half, half, channels).transpose(1, 0, 2).reshape(-1, channels)
    tri_in = tri_in.reshape(2, n, 2, eight, channels).transpose(4, 2, 0, 1, 3)
    return (
        pair_out[None],
        pgrad[None],
        sensitivity[None],
        opm_gain[0, :width],
        opm_proj.reshape(width, 2 * half),
        opm_out,
        bias[0],
        tri_gain[0],
        tri_in.reshape(channels, 4 * channels),
        tri_gate,
        mid_gain[0],
        tri_out,
    )


def solution(mesh):
    placed = (
        P("dp", None, "dap", None),
        P("dp", "dap", None, None),
        P("dp", "dap", None, None),
    ) + (P(),) * 9
    return jax.shard_map(
        local,
        mesh=mesh,
        in_specs=placed,
        out_specs=(
            P("dp", "dap", None, None),
            P("dp", "dap", None, None),
            P("dp", None, "dap", None),
        )
        + (P(),) * 9,
        check_vma=False,
    )
```

```python
import jax
import jax.numpy as jnp
from jax import lax
from jax.experimental import pallas as pl
from jax.experimental.pallas import tpu as pltpu
from jax.sharding import PartitionSpec as P

EPSILON = 1e-05
BF = jnp.bfloat16
F32 = jnp.float32
WIDE = 256


def nn(a, b):
    return lax.dot_general(a, b, (((1,), (0,)), ((), ())), preferred_element_type=F32)


def nt(a, b):
    return lax.dot_general(a, b, (((1,), (1,)), ((), ())), preferred_element_type=F32)


def tn(a, b):
    return lax.dot_general(a, b, (((0,), (0,)), ((), ())), preferred_element_type=F32)


def norm(v):
    centred = v - jnp.mean(v, 0, keepdims=True)
    inverse = lax.rsqrt(jnp.mean(centred * centred, 0, keepdims=True) + EPSILON)
    return centred * inverse, inverse


def norm_back(h, hat, inverse):
    first = jnp.mean(h, 0, keepdims=True)
    second = jnp.mean(h * hat, 0, keepdims=True)
    return (h - first - hat * second) * inverse


def sigmoid(v):
    return 1.0 / (1.0 + jnp.exp(-v))


def pad_rows(v, rows):
    return jnp.concatenate([v, jnp.zeros((rows - v.shape[0],) + v.shape[1:], v.dtype)], 0)


def flip(v):
    return pad_rows(v, WIDE).T


def low_half(v):
    lane = lax.broadcasted_iota(jnp.int32, v.shape, v.ndim - 1)
    return jnp.where(lane < 64, v, 0.0)


def pack(a, b):
    tail = low_half(a[:, 128:]) + pltpu.roll(low_half(b[:, 128:]), 64, 1)
    return a[:, :128], b[:, :128], tail


def unpack(t0, t1, t2):
    return (t0, low_half(t2)), (t1, low_half(pltpu.roll(t2, 64, 1)))


def as_column(row_ref):
    n = row_ref.shape[1]
    a = lax.broadcasted_iota(jnp.int32, (n, n), 0)
    b = lax.broadcasted_iota(jnp.int32, (n, n), 1)
    return jnp.sum(jnp.where(a == b, row_ref[...], 0.0), 1, keepdims=True)


def as_row(column):
    n = column.shape[0]
    a = lax.broadcasted_iota(jnp.int32, (n, n), 0)
    b = lax.broadcasted_iota(jnp.int32, (n, n), 1)
    return jnp.sum(jnp.where(a == b, column, 0.0), 0, keepdims=True)


def call(kernel, outs, scratch, *operands, smem=0, away=0, copies=0):
    specs = [pl.BlockSpec(memory_space=pltpu.SMEM)] * smem
    specs += [pl.BlockSpec(memory_space=pltpu.VMEM)] * (len(operands) - smem)
    room = [pltpu.VMEM(s, t) for s, t in scratch]
    if copies:
        room.append(pltpu.SemaphoreType.DMA((copies,)))
    return pl.pallas_call(
        kernel,
        out_shape=[jax.ShapeDtypeStruct(s, t) for s, t in outs],
        in_specs=specs,
        out_specs=[pl.BlockSpec(memory_space=pltpu.VMEM)] * (len(outs) - away)
        + [pl.BlockSpec(memory_space=pl.ANY)] * away,
        scratch_shapes=room,
        compiler_params=pltpu.CompilerParams(vmem_limit_bytes=50 * 1024 * 1024),
    )(*operands)


def project_kernel(x_ref, gain_ref, w_ref, left_ref, lsend_ref, rsend_ref):
    pairs = x_ref.shape[0]
    width = w_ref.shape[0]
    half = w_ref.shape[1] // 2
    gain = as_column(gain_ref)

    @pl.loop(0, pairs)
    def _(m):
        x = flip(x_ref[m].astype(F32))
        both = []
        for o in range(2):
            hat, _ = norm(x[o * width : (o + 1) * width])
            proj = tn(w_ref[...], (hat * gain).astype(BF))
            both.append(proj)
            left_ref[2 * m + o] = proj[:half].astype(BF)
        for t, v in enumerate(pack(both[0][:half], both[1][:half])):
            lsend_ref[m, t] = v.astype(BF)
        for t, v in enumerate(pack(both[0][half:], both[1][half:])):
            rsend_ref[m, t] = v.astype(BF)


def load_wide(head, tail, start, count, stride):
    a = head[pl.ds(start, count, stride=stride), :]
    b = tail[pl.ds(start, count, stride=stride), :]
    return jnp.concatenate([a, b], 1)


def store_wide(head, tail, start, count, stride, v):
    head[pl.ds(start, count, stride=stride), :] = v[:, :128]
    tail[pl.ds(start, count, stride=stride), :] = v[:, 128:]


def spread_projections(source, first, step, pitch, head, tail):
    pairs, _, half, _ = source.shape
    for m in range(pairs):
        t = source[m].astype(F32)
        for o, (a, b) in enumerate(unpack(t[0], t[1], t[2])):
            at = pl.ds((first + step * (2 * m + o)) * pitch, half)
            head[at, :] = a
            tail[at, :] = b


def outer_kernel(
    par_ref, own_ref, other_ref, left_ref, edge_ref, wt_ref, bias_ref, gain_ref, entry_ref,
    send_ref, mid_ref, normed_ref, right_out, outer_out,
    head, tail, right_ref, outer_ref, sems,
):
    chips, pairs, _, half, _ = own_ref.shape
    rows = left_ref.shape[0]
    length = edge_ref.shape[1]
    depth = 1.0 / length
    pitch = half + 1
    par = par_ref[0]
    for source, p in ((own_ref, par), (other_ref, 1 - par)):

        @pl.loop(0, chips)
        def _(chip):
            spread_projections(source.at[chip], (2 * chip + p) * rows, 1, pitch, head, tail)

    left = left_ref[...].reshape(rows * half, WIDE)

    @pl.loop(0, half, unroll=4)
    def _(q):
        r = pad_rows(load_wide(head, tail, q, length, pitch), WIDE).astype(BF)
        right_ref[q] = r
        o = (nt(left, r) * depth).astype(BF)
        at = pl.ds(pl.multiple_of(q * half, half), half)
        for i in range(rows):
            outer_ref[i, at, :] = o[i * half : (i + 1) * half]

    copies = [
        pltpu.make_async_copy(right_ref, right_out, sems.at[0]),
        pltpu.make_async_copy(outer_ref, outer_out, sems.at[1]),
    ]
    for c in copies:
        c.start()
    devices, _, _, sixteen, _ = send_ref.shape
    bias = as_column(bias_ref)
    gain = as_column(gain_ref)

    @pl.loop(0, pairs)
    def _(m):
        both = []
        for o in range(2):
            i = 2 * m + o
            mid = flip(edge_ref[i].astype(F32)) + (nn(wt_ref[...], outer_ref[i]) + bias)
            mid_ref[i] = mid
            hat, _ = norm(mid)
            normed = (hat * gain).astype(BF)
            normed_ref[i] = normed
            raw = nn(entry_ref[...], normed)
            cut = raw.shape[0] // 2
            both.append(sigmoid(raw[:cut]) * raw[cut:])
        for t, v in enumerate(pack(*both)):
            send_ref[:, m, t] = v.reshape(devices, sixteen, 128).astype(BF)

    for c in copies:
        c.wait()


def gate_kernel(normed_ref, adj_ref, wg_ref, gate_ref, up_ref):
    @pl.loop(0, normed_ref.shape[0])
    def _(i):
        gate_ref[i] = sigmoid(tn(wg_ref[...], normed_ref[i]))
        up_ref[i] = flip(adj_ref[i].astype(F32)).astype(BF)


def spread(source, half, head, tail):
    devices, pairs, _, high, _ = source.shape
    many = high // half

    @pl.loop(0, devices)
    def _(d):
        for m in range(pairs):
            t = source[d, m].astype(F32)
            for o, (a, b) in enumerate(unpack(t[0], t[1], t[2])):
                for g in range(many):
                    at = pl.ds((((d * pairs + m) * 2 + o) * many + g) * (half + 1), half)
                    head[at, :] = a[g * half : (g + 1) * half]
                    tail[at, :] = b[g * half : (g + 1) * half]


def gather_up(half, head, tail, target):
    devices, pairs, _, high, _ = target.shape
    many = high // half

    @pl.loop(0, devices)
    def _(d):
        for m in range(pairs):
            wide = []
            for o in range(2):
                got = []
                for g in range(many):
                    at = pl.ds((((d * pairs + m) * 2 + o) * many + g) * (half + 1), half)
                    got.append(jnp.concatenate([head[at, :], tail[at, :]], 1))
                wide.append(jnp.concatenate(got, 0))
            for t, v in enumerate(pack(*wide)):
                target[d, m, t] = v.astype(BF)


def triangle_kernel(edges_ref, send_ref, left_ref, right_ref, head, tail, mhead, mtail):
    channels, length, _ = left_ref.shape
    spread(edges_ref, 2 * channels, head, tail)
    for c in range(channels):
        a = load_wide(head, tail, c, length, 2 * channels + 1).astype(BF)
        b = load_wide(head, tail, channels + c, length, 2 * channels + 1).astype(BF)
        left_ref[c] = a
        right_ref[c] = b
        mixed = tn(a, b)[:length]
        store_wide(mhead, mtail, c, length, channels + 1, mixed)
    gather_up(channels, mhead, mtail, send_ref)


def triangle_back_kernel(grads_ref, left_ref, right_ref, send_ref, head, tail, mhead, mtail):
    channels, length, _ = left_ref.shape
    spread(grads_ref, channels, mhead, mtail)
    for c in range(channels):
        g = pad_rows(load_wide(mhead, mtail, c, length, channels + 1), WIDE).astype(BF)
        store_wide(head, tail, c, length, 2 * channels + 1, nt(right_ref[c], g))
        store_wide(head, tail, channels + c, length, 2 * channels + 1, nn(left_ref[c], g))
    gather_up(2 * channels, head, tail, send_ref)


def mixed_rows(mixed_ref, n):
    devices, _, _, sixteen, _ = mixed_ref.shape
    eight = sixteen // 2
    t = [mixed_ref[:, n, k].astype(F32).reshape(devices * sixteen, 128) for k in range(3)]
    out = []
    for a, b in unpack(*t):
        block = jnp.concatenate([a, b], 1).reshape(devices, 2, eight, WIDE)
        out += [block[:, o].reshape(devices * eight, WIDE) for o in range(2)]
    return out


def update_kernel(mixed_ref, gate_ref, up_ref, cgain_ref, wf_ref, send_ref):
    devices, quads, _, sixteen, _ = mixed_ref.shape
    cgain = as_column(cgain_ref)

    @pl.loop(0, quads)
    def _(n):
        grads = []
        for k, mixed in enumerate(mixed_rows(mixed_ref, n)):
            i = 4 * n + k
            hat, inverse = norm(mixed)
            gu = (up_ref[i].astype(F32) * gate_ref[i]).astype(BF)
            gmn = nn(wf_ref[...], gu)
            back = norm_back(gmn * cgain, hat, inverse)
            grads.append(back.reshape(devices, 1, sixteen // 2, WIDE))
        packed = [
            jnp.concatenate(grads[2 * o : 2 * o + 2], 1).reshape(devices * sixteen, WIDE)
            for o in range(2)
        ]
        for k, v in enumerate(pack(*packed)):
            send_ref[:, n, k] = v.reshape(devices, sixteen, 128).astype(BF)


def result_kernel(
    mixed_ref, mid_ref, normed_ref, gate_ref, up_ref, cgain_ref, wf_ref,
    out_ref, ggate_ref, wfg_ref, wgg_ref, msum_ref, acc,
):
    _, quads, _, _, _ = mixed_ref.shape
    length = out_ref.shape[1]
    wfg_ref[...] = jnp.zeros_like(wfg_ref)
    wgg_ref[...] = jnp.zeros_like(wgg_ref)
    acc[...] = jnp.zeros_like(acc)
    cgain = as_column(cgain_ref)

    @pl.loop(0, quads)
    def _(n):
        for k, mixed in enumerate(mixed_rows(mixed_ref, n)):
            i = 4 * n + k
            hat, _ = norm(mixed)
            mn = (hat * cgain).astype(BF)
            gate = gate_ref[i]
            update = tn(wf_ref[...], mn)
            new = mid_ref[i] + gate * update
            out_ref[i] = new.T[:length].astype(BF)
            upgate = up_ref[i].astype(F32) * gate
            gu = upgate.astype(BF)
            gg = (upgate * update * (1.0 - gate)).astype(BF)
            ggate_ref[i] = gg
            wfg_ref[...] += nt(mn, gu)
            wgg_ref[...] += nt(normed_ref[i], gg)
            acc[...] += nn(wf_ref[...], gu) * hat

    msum_ref[...] = jnp.sum(acc[...].T, 0, keepdims=True)


def edge_back_kernel(
    grads_ref, mid_ref, normed_ref, ggate_ref, up_ref, gain_ref, entryt_ref, entry_ref, wg_ref,
    pgrad_ref, pgradt_ref, send_ref, win_ref, gsum_ref, bsum_ref, gacc, bacc, rows,
):
    devices, pairs, _, sixteen, _ = grads_ref.shape
    count, length, channels = pgrad_ref.shape
    win_ref[...] = jnp.zeros_like(win_ref)
    gacc[...] = jnp.zeros_like(gacc)
    bacc[...] = jnp.zeros_like(bacc)
    gain = as_column(gain_ref)

    @pl.loop(0, pairs)
    def _(m):
        t = [grads_ref[:, m, k].astype(F32).reshape(devices * sixteen, 128) for k in range(3)]
        for o, (a, b) in enumerate(unpack(*t)):
            i = 2 * m + o
            grad = jnp.concatenate([a, b], 1)
            normed = normed_ref[i]
            raw = nn(entryt_ref[...], normed)
            cut = raw.shape[0] // 2
            sig = sigmoid(raw[:cut])
            gs = grad * sig
            graw = jnp.concatenate([gs * raw[cut:] * (1.0 - sig), gs], 0).astype(BF)
            win_ref[...] += nt(graw, normed)
            gpn = nn(entry_ref[...], graw) + nn(wg_ref[...], ggate_ref[i])
            hat, inverse = norm(mid_ref[i])
            gacc[...] += gpn * hat
            gmid = up_ref[i].astype(F32) + norm_back(gpn * gain, hat, inverse)
            bacc[...] += gmid
            pgradt_ref[i] = gmid.astype(BF)
            turned = gmid.T[:length]
            pgrad_ref[i] = turned.astype(BF)
            rows[pl.ds(i, length, stride=count), :] = turned

    send_ref[...] = rows[...].astype(BF)
    gsum_ref[...] = jnp.sum(gacc[...].T, 0, keepdims=True)
    bsum_ref[...] = jnp.sum(bacc[...].T, 0, keepdims=True)


def prepare_kernel(par_ref, own_ref, other_ref, x_ref, left_ref, hat_ref, inv_ref, head, tail):
    chips, pairs, _, half, _ = own_ref.shape
    length = left_ref.shape[1] * 3 // 4
    devices = 2 * chips
    pitch = half + 1
    par = par_ref[0]
    for source, p in ((own_ref, par), (other_ref, 1 - par)):

        @pl.loop(0, chips)
        def _(chip):
            spread_projections(source.at[chip], 2 * chip + p, devices, pitch, head, tail)

    @pl.loop(0, half, unroll=2)
    def _(q):
        left_ref[q] = pad_rows(load_wide(head, tail, q, length, pitch), WIDE).astype(BF)

    width = hat_ref.shape[1]

    @pl.loop(0, pairs)
    def _(m):
        x = flip(x_ref[m].astype(F32))
        for o in range(2):
            hat, inverse = norm(x[o * width : (o + 1) * width])
            hat_ref[2 * m + o] = hat
            inv_ref[2 * m + o] = inverse


def put(stage, i, g):
    half = g.shape[0] // (stage.shape[0] * (stage.shape[2] // WIDE))
    group = stage.shape[2] // WIDE
    at = pl.ds(pl.multiple_of(i * half, half), half)
    for q in range(g.shape[0] // half):
        lanes = slice((q % group) * WIDE, (q % group + 1) * WIDE)
        stage[q // group, at, lanes] = g[q * half : (q + 1) * half]


def contract(stage, projections, total):
    group = stage.shape[2] // WIDE
    total[...] = jnp.zeros_like(total)

    @pl.loop(0, stage.shape[0], unroll=2)
    def _(k):
        r = projections[pl.ds(k * group, group)].reshape(group * WIDE, WIDE)
        total[...] += nn(stage[k], r)


def squeeze(v):
    n = v.shape[0] // 4
    out = v[:n]
    for k in range(1, 4):
        out = out + pltpu.roll(v[k * n : (k + 1) * n], 32 * k, 1)
    return out


def outer_back_kernel(
    pgradt_ref, right_ref, outer_ref, w_ref, hat_ref, grad_ref, wout_ref, cross_ref,
    stage, wacc, cacc,
):
    count, _, _ = pgradt_ref.shape
    half = right_ref.shape[0]
    depth = 1.0 / (right_ref.shape[1] * 3 // 4)

    wacc[...] = jnp.zeros_like(wacc)

    @pl.loop(0, count // 2)
    def _(m):
        a = jnp.concatenate([outer_ref[2 * m], outer_ref[2 * m + 1]], 1)
        b = jnp.concatenate([pgradt_ref[2 * m], pgradt_ref[2 * m + 1]], 1)
        wacc[...] += nt(a, b)

    for q in range(half):
        wout_ref[pl.ds(q, half, stride=half), :] = wacc[q * half : (q + 1) * half, :]

    @pl.loop(0, count, unroll=2)
    def _(i):
        put(stage, i, nn(w_ref[...], pgradt_ref[i]).astype(BF))

    contract(stage, right_ref, grad_ref)
    grad_ref[...] = grad_ref[...] * depth
    cacc[...] = jnp.zeros_like(cacc)

    @pl.loop(0, count)
    def _(i):
        g = grad_ref[pl.ds(pl.multiple_of(i * half, half), half), :].astype(BF)
        cacc[...] += nt(hat_ref[i].astype(BF), pad_rows(g, 128))

    cross_ref[...] = squeeze(cacc[...])


def column_kernel(
    pcol_ref, left_ref, w_ref, gleft_ref, hat_ref, inv_ref, mgain_ref, wmap_ref,
    out_ref, cross_ref, prow, stage, gright, cacc,
):
    devices, many, channels = pcol_ref.shape
    half = left_ref.shape[0]
    count = gleft_ref.shape[0] // half
    length = devices * count
    pairs = count // 2

    @pl.loop(0, devices)
    def _(d):
        prow[pl.ds(d * (many + 1), many), :] = pcol_ref[d].astype(F32)

    @pl.loop(0, count, unroll=2)
    def _(j):
        p = jnp.concatenate(
            [prow[pl.ds(j * count + i, devices, stride=many + 1), :] for i in range(count)], 0
        )
        put(stage, j, nt(w_ref[...], pad_rows(p, WIDE).astype(BF)).astype(BF))

    contract(stage, left_ref, gright)
    gain = as_column(mgain_ref)
    cacc[...] = jnp.zeros_like(cacc)

    @pl.loop(0, pairs)
    def _(m):
        both = []
        for o in range(2):
            i = 2 * m + o
            hat = hat_ref[i]
            at = pl.ds(pl.multiple_of(i * half, half), half)
            right = (gright[at, :] * (1.0 / length)).astype(BF)
            cacc[...] += nt(hat.astype(BF), pad_rows(right, 128))
            g = jnp.concatenate([gleft_ref[at, :].astype(BF), right], 0)
            both.append(norm_back(nn(wmap_ref[...], g) * gain, hat, inv_ref[i]))
        out_ref[m] = jnp.concatenate(both, 0).T[:length].astype(BF)

    cross_ref[...] = squeeze(cacc[...])


def unsqueeze(v):
    lane = lax.broadcasted_iota(jnp.int32, v.shape, 1)
    got = [v if k == 0 else pltpu.roll(v, 128 - 32 * k, 1) for k in range(4)]
    return jnp.concatenate([jnp.where(lane < 32, g, 0.0) for g in got], 0)


def finish_kernel(
    factor, all_ref, gain_ref, wmap_ref,
    mgain_out, proj_out, wout_out, bias_out, pgain_out, win_out, wgg_out, cgain_out, wfg_out,
    rows, flat,
):
    everyone, each, _ = all_ref.shape
    own = each - 16
    eight = 8

    @pl.loop(0, everyone)
    def _(d):
        rows[pl.ds(pl.multiple_of(d * own, 16), own), :] = all_ref[d, :own].astype(F32) * factor

    many = wout_out.shape[0]
    wout_out[...] = rows[:many, :]
    at = many
    channels = wgg_out.shape[0]
    devices = channels // eight
    for k in range(4):
        lr, gv = k // 2, k % 2
        for d in range(devices):
            start = at + gv * 2 * channels + d * 2 * eight + lr * eight
            flat[d * eight : (d + 1) * eight, :] = rows[start : start + eight, :]
        win_out[:, k * channels : (k + 1) * channels] = flat[...].T
    at += 4 * channels
    wgg_out[...] = rows[at : at + channels, :]
    at += channels
    wfg_out[...] = rows[at : at + channels, :]
    at += channels
    left = unsqueeze(rows[at : at + 16, :])
    at += 16
    cgain_out[...] = rows[at : at + 1, :]
    pgain_out[...] = rows[at + 1 : at + 2, :]
    bias_out[...] = rows[at + 2 : at + 3, :]
    right = unsqueeze(jnp.sum(all_ref[:, own:].astype(F32), 0) * factor)
    width = proj_out.shape[0]
    cross = (left + pltpu.roll(right, 32, 1))[:, :width]
    proj_out[...] = cross * as_column(gain_ref)
    mgain_out[...] = as_row(jnp.sum(cross * wmap_ref[...].astype(F32), 1, keepdims=True))


def exchange(v, axes="dap", groups=None):
    return lax.all_to_all(
        v, axes, split_axis=0, concat_axis=0, tiled=True, axis_index_groups=groups
    )


def local(
    homolog_features,
    edge_features,
    adjoint_edges,
    homolog_scaling_factor,
    tensor_mapping_matrix,
    tensor_final_matrix,
    tensor_final_offset,
    edge_scaling_factor,
    trilateral_entry_matrix,
    final_sigmoid_matrix,
    central_scaling_factor,
    trilateral_final_matrix,
):
    n = lax.axis_size("dap")
    everyone = n * lax.axis_size("dp")
    msa = homolog_features[0]
    depth, count, width = msa.shape
    length = edge_features.shape[2]
    pairs = count // 2
    half = tensor_mapping_matrix.shape[1] // 2
    channels = edge_features.shape[3]
    eight = channels // n
    edges = edge_features[0]
    adjoint = adjoint_edges[0]
    line = lambda v: v.reshape(1, -1)
    msa_gain = line(homolog_scaling_factor)

    x = msa.reshape(depth, pairs, 2 * width).transpose(1, 0, 2)
    left, left_send, right_send = call(
        project_kernel,
        [((count, half, WIDE), BF), ((pairs, 3, half, 128), BF), ((pairs, 3, half, 128), BF)],
        [],
        x, msa_gain, tensor_mapping_matrix,
    )
    chips = n // 2
    groups = [list(range(0, n, 2)), list(range(1, n, 2))]

    def everywhere(v):
        own = exchange(jnp.broadcast_to(v, (chips,) + v.shape), groups=groups)
        return own, lax.ppermute(own, "dap", [(i, i ^ 1) for i in range(n)])

    own, other = everywhere(right_send)
    left_send, other = lax.optimization_barrier((left_send, other))
    left_own, left_other = everywhere(left_send)
    parity = lax.rem(lax.axis_index("dap"), 2).astype(jnp.int32).reshape(1)

    qp = tensor_final_matrix.reshape(half, half, channels).transpose(1, 0, 2)
    qp = qp.reshape(half * half, channels)
    entry = trilateral_entry_matrix.reshape(channels, 2, 2, n, eight).transpose(0, 2, 3, 1, 4)
    entry = entry.reshape(channels, 4 * channels)
    wide = ((count, channels, WIDE), BF)
    wide32 = ((count, channels, WIDE), F32)
    every = ((half, WIDE, WIDE), BF)
    outers = ((count, half * half, WIDE), BF)
    spare = [((length * (half + 1), 128), F32)] * 2
    edge_send, mid, normed, right, outer = call(
        outer_kernel,
        [((n, pairs, 3, 2 * eight, 128), BF), wide32, wide, every, outers],
        spare + [every, outers],
        parity, own, other, left, edges, qp.T, line(tensor_final_offset),
        line(edge_scaling_factor), entry.T, smem=1, away=2, copies=2,
    )
    edge_cols = exchange(edge_send)
    gate, up = call(gate_kernel, [wide32, wide], [], normed, adjoint, final_sigmoid_matrix)
    rooms = [((length * (2 * eight + 1), 128), F32)] * 2
    rooms += [((length * (eight + 1), 128), F32)] * 2
    mixed_send, left_cols, right_cols = call(
        triangle_kernel,
        [((n, pairs // 2, 3, 2 * eight, 128), BF)] + [((eight, length, WIDE), BF)] * 2,
        rooms,
        edge_cols,
    )
    mixed = exchange(mixed_send)
    square = ((channels, channels), F32)
    row = ((1, channels), F32)
    (grad_send,) = call(
        update_kernel,
        [((n, pairs // 2, 3, 2 * eight, 128), BF)],
        [],
        mixed, gate, up, line(central_scaling_factor), trilateral_final_matrix,
    )
    grad_cols = exchange(grad_send)
    pair_out, grad_gate, tri_out, tri_gate, mid_gain = call(
        result_kernel,
        [(edges.shape, BF), wide, square, square, row],
        [((channels, WIDE), F32)],
        mixed, mid, normed, gate, up, line(central_scaling_factor), trilateral_final_matrix,
    )
    (back_send,) = call(
        triangle_back_kernel,
        [((n, pairs, 3, 2 * eight, 128), BF)],
        rooms,
        grad_cols, left_cols, right_cols,
    )
    back = exchange(back_send)
    left_own, left_other, back_send = lax.optimization_barrier((left_own, left_other, back_send))
    lefts, hat, inverse = call(
        prepare_kernel,
        [every, ((count, width, WIDE), F32), ((count, 1, WIDE), F32)],
        spare,
        parity, left_own, left_other, x, smem=1,
    )
    pgrad, pgradt, pgrad_send, tri_in, tri_gain, bias = call(
        edge_back_kernel,
        [
            (edges.shape, BF), wide, ((length * count, channels), BF),
            ((4 * channels, channels), F32), row, row,
        ],
        [((channels, WIDE), F32)] * 2 + [((length * count, channels), F32)],
        back, mid, normed, grad_gate, up, line(edge_scaling_factor),
        entry.T, entry, final_sigmoid_matrix,
    )
    pgrad_cols = exchange(pgrad_send.reshape(n, count * count, channels))
    group = 4
    stage = ((half // group, count * half, group * WIDE), BF)
    grads = ((count * half, WIDE), F32)
    cross = ((width // 4, 128), F32)
    full = ((half * half, channels), F32)
    grad_left, opm_out, cross_left = call(
        outer_back_kernel,
        [grads, full, cross],
        [stage, full, ((width, 128), F32)],
        pgradt, right, outer, qp, hat,
    )
    parts = [opm_out, tri_in, tri_gate, tri_out, cross_left, mid_gain, tri_gain, bias]
    used = sum(p.shape[0] for p in parts)
    each = -(-used // (16 * everyone)) * 16
    parts.append(jnp.zeros((each * everyone - used, 128), F32))
    mine = exchange(
        jnp.concatenate(parts, 0).astype(BF).reshape(everyone, each, 128), ("dp", "dap")
    )
    sens, cross_right = call(
        column_kernel,
        [((pairs, length, 2 * width), BF), cross],
        [((devices_rows(n, count), channels), F32), stage, grads, ((width, 128), F32)],
        pgrad_cols, lefts, tensor_final_matrix, grad_left, hat, inverse,
        msa_gain, tensor_mapping_matrix,
    )
    sensitivity = sens.transpose(1, 0, 2).reshape(depth, count, width)
    mine = jnp.sum(mine.astype(F32), 0)
    mine = jnp.concatenate([mine, cross_right], 0).astype(BF)
    total = exchange(jnp.broadcast_to(mine, (everyone, each + 16, 128)), ("dp", "dap"))
    factor = 1.0 / (lax.axis_size("dp") * length)
    last = call(
        lambda *refs: finish_kernel(factor, *refs),
        [
            ((1, width), F32), ((width, 2 * half), F32), full, row, row,
            ((channels, 4 * channels), F32), square, row, square,
        ],
        [((everyone * each, 128), F32), ((channels, 128), F32)],
        total, msa_gain, tensor_mapping_matrix,
    )
    last = [v.reshape(-1) if v.shape[0] == 1 else v for v in last]
    return (pair_out[None], pgrad[None], sensitivity[None], *last)


def devices_rows(devices, count):
    return devices * (count * count + 1)


def solution(mesh):
    placed = (
        P("dp", None, "dap", None),
        P("dp", "dap", None, None),
        P("dp", "dap", None, None),
    ) + (P(),) * 9
    return jax.shard_map(
        local,
        mesh=mesh,
        in_specs=placed,
        out_specs=(
            P("dp", "dap", None, None),
            P("dp", "dap", None, None),
            P("dp", None, "dap", None),
        )
        + (P(),) * 9,
        check_vma=False,
    )
```

```python
import jax
import jax.numpy as jnp
from jax import lax
from jax.experimental import pallas as pl
from jax.experimental.pallas import tpu as pltpu
from jax.sharding import PartitionSpec as P

EPSILON = 1e-05
BF = jnp.bfloat16
F32 = jnp.float32
WIDE = 256


def nn(a, b):
    return lax.dot_general(a, b, (((1,), (0,)), ((), ())), preferred_element_type=F32)


def nt(a, b):
    return lax.dot_general(a, b, (((1,), (1,)), ((), ())), preferred_element_type=F32)


def tn(a, b):
    return lax.dot_general(a, b, (((0,), (0,)), ((), ())), preferred_element_type=F32)


def norm(v):
    centred = v - jnp.mean(v, 0, keepdims=True)
    inverse = lax.rsqrt(jnp.mean(centred * centred, 0, keepdims=True) + EPSILON)
    return centred * inverse, inverse


def norm_back(h, hat, inverse):
    first = jnp.mean(h, 0, keepdims=True)
    second = jnp.mean(h * hat, 0, keepdims=True)
    return (h - first - hat * second) * inverse


def sigmoid(v):
    return 1.0 / (1.0 + jnp.exp(-v))


def pad_rows(v, rows):
    return jnp.concatenate([v, jnp.zeros((rows - v.shape[0],) + v.shape[1:], v.dtype)], 0)


def flip(v):
    return pad_rows(v, WIDE).T


def low_half(v):
    lane = lax.broadcasted_iota(jnp.int32, v.shape, v.ndim - 1)
    return jnp.where(lane < 64, v, 0.0)


def pack(a, b):
    tail = low_half(a[:, 128:]) + pltpu.roll(low_half(b[:, 128:]), 64, 1)
    return a[:, :128], b[:, :128], tail


def unpack(t0, t1, t2):
    return (t0, low_half(t2)), (t1, low_half(pltpu.roll(t2, 64, 1)))


def as_column(row_ref):
    n = row_ref.shape[1]
    a = lax.broadcasted_iota(jnp.int32, (n, n), 0)
    b = lax.broadcasted_iota(jnp.int32, (n, n), 1)
    return jnp.sum(jnp.where(a == b, row_ref[...], 0.0), 1, keepdims=True)


def as_row(column):
    n = column.shape[0]
    a = lax.broadcasted_iota(jnp.int32, (n, n), 0)
    b = lax.broadcasted_iota(jnp.int32, (n, n), 1)
    return jnp.sum(jnp.where(a == b, column, 0.0), 0, keepdims=True)


def call(us, kernel, outs, scratch, *operands, smem=0, away=0, sems=None):
    specs = [pl.BlockSpec(memory_space=pltpu.SMEM)] * smem
    specs += [pl.BlockSpec(memory_space=pltpu.VMEM)] * (len(operands) - smem)
    room = [pltpu.VMEM(s, t) for s, t in scratch]
    if away:
        room.append(pltpu.SemaphoreType.DMA(sems or (away,)))
    return pl.pallas_call(
        kernel,
        out_shape=[jax.ShapeDtypeStruct(s, t) for s, t in outs],
        in_specs=specs,
        out_specs=[pl.BlockSpec(memory_space=pltpu.VMEM)] * (len(outs) - away)
        + [pl.BlockSpec(memory_space=pltpu.HBM)] * away,
        scratch_shapes=room,
        compiler_params=pltpu.CompilerParams(vmem_limit_bytes=50 * 1024 * 1024),
        cost_estimate=pl.CostEstimate(flops=us * 10**9, bytes_accessed=0, transcendentals=0),
    )(*operands)


def project_kernel(
    x_ref, gain_ref, w_ref, left_ref, rsend_out, lsend_out, rsend_ref, lsend_ref, sems
):
    pairs = x_ref.shape[0]
    width = w_ref.shape[0]
    half = w_ref.shape[1] // 2
    gain = as_column(gain_ref)

    @pl.loop(0, pairs, unroll=3)
    def _(m):
        x = flip(x_ref[m].astype(F32))
        both = []
        for o in range(2):
            hat, _ = norm(x[o * width : (o + 1) * width])
            proj = tn(w_ref[...], (hat * gain).astype(BF))
            both.append(proj)
            left_ref[2 * m + o] = proj[:half].astype(BF)
        for t, v in enumerate(pack(both[0][:half], both[1][:half])):
            lsend_ref[m, t] = v.astype(BF)
        for t, v in enumerate(pack(both[0][half:], both[1][half:])):
            rsend_ref[m, t] = v.astype(BF)

    copies = []
    for k in range(rsend_out.shape[0]):
        copies.append(pltpu.make_async_copy(rsend_ref, rsend_out.at[k], sems.at[0, k]))
        copies.append(pltpu.make_async_copy(lsend_ref, lsend_out.at[k], sems.at[1, k]))
    for c in copies:
        c.start()
    for c in copies:
        c.wait()


def load_wide(head, tail, start, count, stride):
    a = head[pl.ds(start, count, stride=stride), :]
    b = tail[pl.ds(start, count, stride=stride), :]
    return jnp.concatenate([a, b], 1)


def store_wide(head, tail, start, count, stride, v):
    head[pl.ds(start, count, stride=stride), :] = v[:, :128]
    tail[pl.ds(start, count, stride=stride), :] = v[:, 128:]


def spread_projections(source, first, step, pitch, head, tail):
    pairs, _, half, _ = source.shape
    for m in range(pairs):
        t = source[m].astype(F32)
        for o, (a, b) in enumerate(unpack(t[0], t[1], t[2])):
            at = pl.ds((first + step * (2 * m + o)) * pitch, half)
            head[at, :] = a
            tail[at, :] = b


def outer_kernel(
    par_ref, own_ref, other_ref, left_ref, edge_ref, wt_ref, bias_ref, gain_ref, entry_ref,
    send_ref, mid_ref, normed_ref, right_out, outer_out,
    head, tail, right_ref, outer_ref, sems,
):
    chips, pairs, _, half, _ = own_ref.shape
    rows = left_ref.shape[0]
    length = edge_ref.shape[1]
    depth = 1.0 / length
    pitch = half + 1
    par = par_ref[0]
    for source, p in ((own_ref, par), (other_ref, 1 - par)):

        @pl.loop(0, chips)
        def _(chip):
            spread_projections(source.at[chip], (2 * chip + p) * rows, 1, pitch, head, tail)

    left = left_ref[...].reshape(rows * half, WIDE)

    @pl.loop(0, half, unroll=4)
    def _(q):
        r = pad_rows(load_wide(head, tail, q, length, pitch), WIDE).astype(BF)
        right_ref[q] = r
        o = (nt(left, r) * depth).astype(BF)
        at = pl.ds(pl.multiple_of(q * half, half), half)
        for i in range(rows):
            outer_ref[i, at, :] = o[i * half : (i + 1) * half]

    copies = [
        pltpu.make_async_copy(right_ref, right_out, sems.at[0]),
        pltpu.make_async_copy(outer_ref, outer_out, sems.at[1]),
    ]
    for c in copies:
        c.start()
    devices, _, _, sixteen, _ = send_ref.shape
    bias = as_column(bias_ref)
    gain = as_column(gain_ref)

    @pl.loop(0, pairs, unroll=3)
    def _(m):
        both = []
        for o in range(2):
            i = 2 * m + o
            mid = flip(edge_ref[i].astype(F32)) + (nn(wt_ref[...], outer_ref[i]) + bias)
            mid_ref[i] = mid
            hat, _ = norm(mid)
            normed = (hat * gain).astype(BF)
            normed_ref[i] = normed
            raw = nn(entry_ref[...], normed)
            cut = raw.shape[0] // 2
            both.append(sigmoid(raw[:cut]) * raw[cut:])
        for t, v in enumerate(pack(*both)):
            send_ref[:, m, t] = v.reshape(devices, sixteen, 128).astype(BF)

    for c in copies:
        c.wait()


def gate_kernel(normed_ref, adj_ref, wg_ref, gate_ref, up_ref):
    @pl.loop(0, normed_ref.shape[0])
    def _(i):
        gate_ref[i] = sigmoid(tn(wg_ref[...], normed_ref[i]))
        up_ref[i] = flip(adj_ref[i].astype(F32)).astype(BF)


def spread(source, half, head, tail):
    devices, pairs, _, high, _ = source.shape
    many = high // half

    @pl.loop(0, devices)
    def _(d):
        for m in range(pairs):
            t = source[d, m].astype(F32)
            for o, (a, b) in enumerate(unpack(t[0], t[1], t[2])):
                for g in range(many):
                    at = pl.ds((((d * pairs + m) * 2 + o) * many + g) * (half + 1), half)
                    head[at, :] = a[g * half : (g + 1) * half]
                    tail[at, :] = b[g * half : (g + 1) * half]


def gather_up(half, head, tail, target):
    devices, pairs, _, high, _ = target.shape
    many = high // half

    @pl.loop(0, devices)
    def _(d):
        for m in range(pairs):
            wide = []
            for o in range(2):
                got = []
                for g in range(many):
                    at = pl.ds((((d * pairs + m) * 2 + o) * many + g) * (half + 1), half)
                    got.append(jnp.concatenate([head[at, :], tail[at, :]], 1))
                wide.append(jnp.concatenate(got, 0))
            for t, v in enumerate(pack(*wide)):
                target[d, m, t] = v.astype(BF)


def triangle_kernel(
    edges_ref, send_ref, left_out, right_out, head, tail, mhead, mtail, left_ref, right_ref, sems
):
    channels, length, _ = left_ref.shape
    spread(edges_ref, 2 * channels, head, tail)
    for c in range(channels):
        a = load_wide(head, tail, c, length, 2 * channels + 1).astype(BF)
        b = load_wide(head, tail, channels + c, length, 2 * channels + 1).astype(BF)
        left_ref[c] = a
        right_ref[c] = b
        mixed = tn(a, b)[:length]
        store_wide(mhead, mtail, c, length, channels + 1, mixed)
    copies = [
        pltpu.make_async_copy(left_ref, left_out, sems.at[0]),
        pltpu.make_async_copy(right_ref, right_out, sems.at[1]),
    ]
    for c in copies:
        c.start()
    gather_up(channels, mhead, mtail, send_ref)
    for c in copies:
        c.wait()


def triangle_back_kernel(grads_ref, left_ref, right_ref, send_ref, head, tail, mhead, mtail):
    channels, length, _ = left_ref.shape
    spread(grads_ref, channels, mhead, mtail)
    for c in range(channels):
        g = pad_rows(load_wide(mhead, mtail, c, length, channels + 1), WIDE).astype(BF)
        store_wide(head, tail, c, length, 2 * channels + 1, nt(right_ref[c], g))
        store_wide(head, tail, channels + c, length, 2 * channels + 1, nn(left_ref[c], g))
    gather_up(2 * channels, head, tail, send_ref)


def mixed_rows(mixed_ref, n):
    devices, _, _, sixteen, _ = mixed_ref.shape
    eight = sixteen // 2
    t = [mixed_ref[:, n, k].astype(F32).reshape(devices * sixteen, 128) for k in range(3)]
    out = []
    for a, b in unpack(*t):
        block = jnp.concatenate([a, b], 1).reshape(devices, 2, eight, WIDE)
        out += [block[:, o].reshape(devices * eight, WIDE) for o in range(2)]
    return out


def update_kernel(mixed_ref, gate_ref, up_ref, cgain_ref, wf_ref, send_ref):
    devices, quads, _, sixteen, _ = mixed_ref.shape
    cgain = as_column(cgain_ref)

    @pl.loop(0, quads, unroll=3)
    def _(n):
        grads = []
        for k, mixed in enumerate(mixed_rows(mixed_ref, n)):
            i = 4 * n + k
            hat, inverse = norm(mixed)
            gu = (up_ref[i].astype(F32) * gate_ref[i]).astype(BF)
            gmn = nn(wf_ref[...], gu)
            back = norm_back(gmn * cgain, hat, inverse)
            grads.append(back.reshape(devices, 1, sixteen // 2, WIDE))
        packed = [
            jnp.concatenate(grads[2 * o : 2 * o + 2], 1).reshape(devices * sixteen, WIDE)
            for o in range(2)
        ]
        for k, v in enumerate(pack(*packed)):
            send_ref[:, n, k] = v.reshape(devices, sixteen, 128).astype(BF)


def result_kernel(
    mixed_ref, mid_ref, normed_ref, gate_ref, up_ref, cgain_ref, wf_ref,
    out_ref, ggate_ref, wfg_ref, wgg_ref, msum_ref, acc,
):
    _, quads, _, _, _ = mixed_ref.shape
    length = out_ref.shape[1]
    wfg_ref[...] = jnp.zeros_like(wfg_ref)
    wgg_ref[...] = jnp.zeros_like(wgg_ref)
    acc[...] = jnp.zeros_like(acc)
    cgain = as_column(cgain_ref)

    @pl.loop(0, quads)
    def _(n):
        for k, mixed in enumerate(mixed_rows(mixed_ref, n)):
            i = 4 * n + k
            hat, _ = norm(mixed)
            mn = (hat * cgain).astype(BF)
            gate = gate_ref[i]
            update = tn(wf_ref[...], mn)
            new = mid_ref[i] + gate * update
            out_ref[i] = new.T[:length].astype(BF)
            upgate = up_ref[i].astype(F32) * gate
            gu = upgate.astype(BF)
            gg = (upgate * update * (1.0 - gate)).astype(BF)
            ggate_ref[i] = gg
            wfg_ref[...] += nt(mn, gu)
            wgg_ref[...] += nt(normed_ref[i], gg)
            acc[...] += nn(wf_ref[...], gu) * hat

    msum_ref[...] = jnp.sum(acc[...].T, 0, keepdims=True)


def edge_back_kernel(
    grads_ref, mid_ref, normed_ref, ggate_ref, up_ref, gain_ref, entryt_ref, entry_ref, wg_ref,
    pgrad_ref, pgradt_ref, send_ref, win_ref, gsum_ref, bsum_ref, gacc, bacc, rows,
):
    devices, pairs, _, sixteen, _ = grads_ref.shape
    count, length, channels = pgrad_ref.shape
    win_ref[...] = jnp.zeros_like(win_ref)
    gacc[...] = jnp.zeros_like(gacc)
    bacc[...] = jnp.zeros_like(bacc)
    gain = as_column(gain_ref)

    @pl.loop(0, pairs, unroll=3)
    def _(m):
        t = [grads_ref[:, m, k].astype(F32).reshape(devices * sixteen, 128) for k in range(3)]
        for o, (a, b) in enumerate(unpack(*t)):
            i = 2 * m + o
            grad = jnp.concatenate([a, b], 1)
            normed = normed_ref[i]
            raw = nn(entryt_ref[...], normed)
            cut = raw.shape[0] // 2
            sig = sigmoid(raw[:cut])
            gs = grad * sig
            graw = jnp.concatenate([gs * raw[cut:] * (1.0 - sig), gs], 0).astype(BF)
            win_ref[...] += nt(graw, normed)
            gpn = nn(entry_ref[...], graw) + nn(wg_ref[...], ggate_ref[i])
            hat, inverse = norm(mid_ref[i])
            gacc[...] += gpn * hat
            gmid = up_ref[i].astype(F32) + norm_back(gpn * gain, hat, inverse)
            bacc[...] += gmid
            pgradt_ref[i] = gmid.astype(BF)
            turned = gmid.T[:length]
            pgrad_ref[i] = turned.astype(BF)
            rows[pl.ds(i, length, stride=count), :] = turned

    send_ref[...] = rows[...].astype(BF)
    gsum_ref[...] = jnp.sum(gacc[...].T, 0, keepdims=True)
    bsum_ref[...] = jnp.sum(bacc[...].T, 0, keepdims=True)


def prepare_kernel(par_ref, own_ref, other_ref, x_ref, left_ref, hat_ref, inv_ref, head, tail):
    chips, pairs, _, half, _ = own_ref.shape
    length = left_ref.shape[1] * 3 // 4
    devices = 2 * chips
    pitch = half + 1
    par = par_ref[0]
    for source, p in ((own_ref, par), (other_ref, 1 - par)):

        @pl.loop(0, chips)
        def _(chip):
            spread_projections(source.at[chip], 2 * chip + p, devices, pitch, head, tail)

    @pl.loop(0, half, unroll=2)
    def _(q):
        left_ref[q] = pad_rows(load_wide(head, tail, q, length, pitch), WIDE).astype(BF)

    width = hat_ref.shape[1]

    @pl.loop(0, pairs)
    def _(m):
        x = flip(x_ref[m].astype(F32))
        for o in range(2):
            hat, inverse = norm(x[o * width : (o + 1) * width])
            hat_ref[2 * m + o] = hat
            inv_ref[2 * m + o] = inverse


def put(stage, i, g):
    half = g.shape[0] // (stage.shape[0] * (stage.shape[2] // WIDE))
    group = stage.shape[2] // WIDE
    at = pl.ds(pl.multiple_of(i * half, half), half)
    for q in range(g.shape[0] // half):
        lanes = slice((q % group) * WIDE, (q % group + 1) * WIDE)
        stage[q // group, at, lanes] = g[q * half : (q + 1) * half]


def contract(stage, projections, total):
    group = stage.shape[2] // WIDE
    total[...] = jnp.zeros_like(total)

    @pl.loop(0, stage.shape[0], unroll=2)
    def _(k):
        r = projections[pl.ds(k * group, group)].reshape(group * WIDE, WIDE)
        total[...] += nn(stage[k], r)


def weight_kernel(
    pgradt_ref, outer_ref, win_ref, wgg_ref, wfg_ref, cgain_ref, pgain_ref, bias_ref,
    out_ref, wacc, wout,
):
    count = pgradt_ref.shape[0]
    many = wacc.shape[0]
    half = out_ref.shape[1] // 4
    wacc[...] = jnp.zeros_like(wacc)

    @pl.loop(0, count // 2, unroll=2)
    def _(m):
        a = jnp.concatenate([outer_ref[2 * m], outer_ref[2 * m + 1]], 1)
        b = jnp.concatenate([pgradt_ref[2 * m], pgradt_ref[2 * m + 1]], 1)
        wacc[...] += nt(a, b)

    for q in range(half):
        wout[pl.ds(q, half, stride=half + 1), :] = wacc[q * half : (q + 1) * half, :]
    for p in range(half):
        out_ref[p * half : (p + 1) * half, :] = wout[
            p * (half + 1) : p * (half + 1) + half, :
        ].astype(BF)
    at = many
    for ref in (win_ref, wgg_ref, wfg_ref):
        out_ref[at : at + ref.shape[0], :] = ref[...].astype(BF)
        at += ref.shape[0]
    rest = [cgain_ref[...], pgain_ref[...], bias_ref[...], jnp.zeros((13, 128), F32)]
    out_ref[at : at + 16, :] = jnp.concatenate(rest, 0).astype(BF)
    at += 16
    out_ref[at:, :] = jnp.zeros((out_ref.shape[0] - at, 128), BF)


def outer_back_kernel(pgradt_ref, right_ref, w_ref, grad_ref, stage):
    count, _, _ = pgradt_ref.shape
    depth = 1.0 / (right_ref.shape[1] * 3 // 4)

    @pl.loop(0, count, unroll=2)
    def _(i):
        put(stage, i, nn(w_ref[...], pgradt_ref[i]).astype(BF))

    contract(stage, right_ref, grad_ref)
    grad_ref[...] = grad_ref[...] * depth


def column_kernel(
    pcol_ref, left_ref, w_ref, gleft_ref, hat_ref, inv_ref, mgain_ref, wmap_ref,
    out_ref, cross_ref, prow, stage, gright, cacc,
):
    devices, many, channels = pcol_ref.shape
    half = left_ref.shape[0]
    count = gleft_ref.shape[0] // half
    length = devices * count
    pairs = count // 2

    @pl.loop(0, devices)
    def _(d):
        prow[pl.ds(d * (many + 1), many), :] = pcol_ref[d].astype(F32)

    @pl.loop(0, count, unroll=2)
    def _(j):
        p = jnp.concatenate(
            [prow[pl.ds(j * count + i, devices, stride=many + 1), :] for i in range(count)], 0
        )
        put(stage, j, nt(w_ref[...], pad_rows(p, WIDE).astype(BF)).astype(BF))

    contract(stage, left_ref, gright)
    gain = as_column(mgain_ref)
    cacc[...] = jnp.zeros_like(cacc)

    @pl.loop(0, pairs, unroll=3)
    def _(m):
        both = []
        for o in range(2):
            i = 2 * m + o
            hat = hat_ref[i]
            at = pl.ds(pl.multiple_of(i * half, half), half)
            right = (gright[at, :] * (1.0 / length)).astype(BF)
            g = jnp.concatenate([gleft_ref[at, :].astype(BF), right], 0)
            cacc[...] += nt(hat.astype(BF), pad_rows(g, 128))
            both.append(norm_back(nn(wmap_ref[...], g) * gain, hat, inv_ref[i]))
        out_ref[m] = jnp.concatenate(both, 0).T[:length].astype(BF)

    rows = cross_ref.shape[0]
    cross_ref[...] = (cacc[:rows, :] + pltpu.roll(cacc[rows:, :], 64, 1)).astype(BF)


def finish_kernel(
    factor, all_ref, gain_ref, wmap_ref,
    mgain_out, proj_out, wout_out, bias_out, pgain_out, win_out, wgg_out, cgain_out, wfg_out,
    rows, flat,
):
    everyone, each, _ = all_ref.shape
    width = proj_out.shape[0]
    own = each - width // 2
    eight = 8

    @pl.loop(0, everyone)
    def _(d):
        rows[pl.ds(pl.multiple_of(d * own, 16), own), :] = all_ref[d, :own].astype(F32) * factor

    many = wout_out.shape[0]
    wout_out[...] = rows[:many, :]
    at = many
    channels = wgg_out.shape[0]
    devices = channels // eight
    for k in range(4):
        lr, gv = k // 2, k % 2
        for d in range(devices):
            start = at + gv * 2 * channels + d * 2 * eight + lr * eight
            flat[d * eight : (d + 1) * eight, :] = rows[start : start + eight, :]
        win_out[:, k * channels : (k + 1) * channels] = flat[...].T
    at += 4 * channels
    wgg_out[...] = rows[at : at + channels, :]
    at += channels
    wfg_out[...] = rows[at : at + channels, :]
    at += channels
    cgain_out[...] = rows[at : at + 1, :]
    pgain_out[...] = rows[at + 1 : at + 2, :]
    bias_out[...] = rows[at + 2 : at + 3, :]
    cross = jnp.sum(all_ref[:, own:].astype(F32), 0) * factor
    cross = jnp.concatenate([cross, pltpu.roll(cross, 64, 1)], 0)[:, :width]
    proj_out[...] = cross * as_column(gain_ref)
    mgain_out[...] = as_row(jnp.sum(cross * wmap_ref[...].astype(F32), 1, keepdims=True))


def exchange(v, axes="dap", groups=None):
    return lax.all_to_all(
        v, axes, split_axis=0, concat_axis=0, tiled=True, axis_index_groups=groups
    )


def local(
    homolog_features,
    edge_features,
    adjoint_edges,
    homolog_scaling_factor,
    tensor_mapping_matrix,
    tensor_final_matrix,
    tensor_final_offset,
    edge_scaling_factor,
    trilateral_entry_matrix,
    final_sigmoid_matrix,
    central_scaling_factor,
    trilateral_final_matrix,
):
    n = lax.axis_size("dap")
    msa = homolog_features[0]
    depth, count, width = msa.shape
    length = edge_features.shape[2]
    pairs = count // 2
    half = tensor_mapping_matrix.shape[1] // 2
    channels = edge_features.shape[3]
    eight = channels // n
    edges = edge_features[0]
    adjoint = adjoint_edges[0]
    line = lambda v: v.reshape(1, -1)
    msa_gain = line(homolog_scaling_factor)

    x = msa.reshape(depth, pairs, 2 * width).transpose(1, 0, 2)
    chips = n // 2
    left, right_send, left_send = call(
        2,
        project_kernel,
        [((count, half, WIDE), BF)] + [((chips, pairs, 3, half, 128), BF)] * 2,
        [((pairs, 3, half, 128), BF)] * 2,
        x, msa_gain, tensor_mapping_matrix,
        away=2, sems=(2, chips),
    )
    groups = [list(range(0, n, 2)), list(range(1, n, 2))]

    def sibling(v):
        return lax.ppermute(v, "dap", [(i, i ^ 1) for i in range(n)])

    own = exchange(right_send, groups=groups)
    other = sibling(own)
    left_send, other = lax.optimization_barrier((left_send, other))
    left_own = exchange(left_send, groups=groups)
    parity = lax.rem(lax.axis_index("dap"), 2).astype(jnp.int32).reshape(1)

    qp = tensor_final_matrix.reshape(half, half, channels).transpose(1, 0, 2)
    qp = qp.reshape(half * half, channels)
    entry = trilateral_entry_matrix.reshape(channels, 2, 2, n, eight).transpose(0, 2, 3, 1, 4)
    entry = entry.reshape(channels, 4 * channels)
    wide = ((count, channels, WIDE), BF)
    wide32 = ((count, channels, WIDE), F32)
    every = ((half, WIDE, WIDE), BF)
    outers = ((count, half * half, WIDE), BF)
    spare = [((length * (half + 1), 128), F32)] * 2
    edge_send, mid, normed, right, outer = call(
        14,
        outer_kernel,
        [((n, pairs, 3, 2 * eight, 128), BF), wide32, wide, every, outers],
        spare + [every, outers],
        parity, own, other, left, edges, qp.T, line(tensor_final_offset),
        line(edge_scaling_factor), entry.T, smem=1, away=2,
    )
    edge_send, left_own = lax.optimization_barrier((edge_send, left_own))
    edge_cols = exchange(edge_send)
    left_other = sibling(left_own)
    gate, up = call(3, gate_kernel, [wide32, wide], [], normed, adjoint, final_sigmoid_matrix)
    rooms = [((length * (2 * eight + 1), 128), F32)] * 2
    rooms += [((length * (eight + 1), 128), F32)] * 2
    mixed_send, left_cols, right_cols = call(
        3,
        triangle_kernel,
        [((n, pairs // 2, 3, 2 * eight, 128), BF)] + [((eight, length, WIDE), BF)] * 2,
        rooms + [((eight, length, WIDE), BF)] * 2,
        edge_cols,
        away=2,
    )
    mixed_send, gate, up = lax.optimization_barrier((mixed_send, gate, up))
    mixed = exchange(mixed_send)
    square = ((channels, channels), F32)
    row = ((1, channels), F32)
    (grad_send,) = call(
        2,
        update_kernel,
        [((n, pairs // 2, 3, 2 * eight, 128), BF)],
        [],
        mixed, gate, up, line(central_scaling_factor), trilateral_final_matrix,
    )
    grad_cols = exchange(grad_send)
    pair_out, grad_gate, tri_out, tri_gate, mid_gain = call(
        6,
        result_kernel,
        [(edges.shape, BF), wide, square, square, row],
        [((channels, WIDE), F32)],
        mixed, mid, normed, gate, up, line(central_scaling_factor), trilateral_final_matrix,
    )
    (back_send,) = call(
        4,
        triangle_back_kernel,
        [((n, pairs, 3, 2 * eight, 128), BF)],
        rooms,
        grad_cols, left_cols, right_cols,
    )
    back = exchange(back_send)
    left_own, left_other, back_send = lax.optimization_barrier((left_own, left_other, back_send))
    lefts, hat, inverse = call(
        6,
        prepare_kernel,
        [every, ((count, width, WIDE), F32), ((count, 1, WIDE), F32)],
        spare,
        parity, left_own, left_other, x, smem=1,
    )
    pgrad, pgradt, pgrad_send, tri_in, tri_gain, bias = call(
        9,
        edge_back_kernel,
        [
            (edges.shape, BF), wide, ((length * count, channels), BF),
            ((4 * channels, channels), F32), row, row,
        ],
        [((channels, WIDE), F32)] * 2 + [((length * count, channels), F32)],
        back, mid, normed, grad_gate, up, line(edge_scaling_factor),
        entry.T, entry, final_sigmoid_matrix,
    )
    pgrad_cols = exchange(pgrad_send.reshape(n, count * count, channels))
    group = 4
    stage = ((half // group, count * half, group * WIDE), BF)
    grads = ((count * half, WIDE), F32)
    cross = ((width // 2, 128), BF)
    full = ((half * half, channels), F32)
    used = half * half + 6 * channels + 3
    each = -(-used // (16 * n)) * 16
    (weights,) = call(
        6,
        weight_kernel,
        [((each * n, channels), BF)],
        [full, ((half * (half + 1), channels), F32)],
        pgradt, outer, tri_in, tri_gate, tri_out, mid_gain, tri_gain, bias,
    )
    (grad_left,) = call(7, outer_back_kernel, [grads], [stage], pgradt, right, qp)
    weights, pgrad_cols = lax.optimization_barrier((weights, pgrad_cols))
    mine = exchange(weights.reshape(n, each, channels))
    sens, cross = call(
        9,
        column_kernel,
        [((pairs, length, 2 * width), BF), cross],
        [((devices_rows(n, count), channels), F32), stage, grads, ((width, 128), F32)],
        pgrad_cols, lefts, tensor_final_matrix, grad_left, hat, inverse,
        msa_gain, tensor_mapping_matrix,
    )
    sensitivity = sens.transpose(1, 0, 2).reshape(depth, count, width)
    crops = lax.axis_size("dp")
    mine = jnp.concatenate([jnp.sum(mine.astype(F32), 0).astype(BF), cross], 0)
    mine = exchange(jnp.broadcast_to(mine, (crops,) + mine.shape), "dp")
    mine = jnp.sum(mine.astype(F32), 0).astype(BF)
    total = exchange(jnp.broadcast_to(mine, (n,) + mine.shape))
    factor = 1.0 / (crops * length)
    last = call(
        2,
        lambda *refs: finish_kernel(factor, *refs),
        [
            ((1, width), F32), ((width, 2 * half), F32), full, row, row,
            ((channels, 4 * channels), F32), square, row, square,
        ],
        [((n * each, 128), F32), ((channels, 128), F32)],
        total, msa_gain, tensor_mapping_matrix,
    )
    last = [v.reshape(-1) if v.shape[0] == 1 else v for v in last]
    return (pair_out[None], pgrad[None], sensitivity[None], *last)


def devices_rows(devices, count):
    return devices * (count * count + 1)


def solution(mesh):
    placed = (
        P("dp", None, "dap", None),
        P("dp", "dap", None, None),
        P("dp", "dap", None, None),
    ) + (P(),) * 9
    return jax.shard_map(
        local,
        mesh=mesh,
        in_specs=placed,
        out_specs=(
            P("dp", "dap", None, None),
            P("dp", "dap", None, None),
            P("dp", None, "dap", None),
        )
        + (P(),) * 9,
        check_vma=False,
    )
```

```python
import math

import jax
import jax.numpy as jnp
from jax import lax
from jax.experimental import pallas as pl
from jax.experimental.pallas import tpu as pltpu
from jax.sharding import PartitionSpec as P

EPSILON = 1e-05
BF = jnp.bfloat16
F32 = jnp.float32
WIDE = 256


def nn(a, b):
    return lax.dot_general(a, b, (((1,), (0,)), ((), ())), preferred_element_type=F32)


def nt(a, b):
    return lax.dot_general(a, b, (((1,), (1,)), ((), ())), preferred_element_type=F32)


def tn(a, b):
    return lax.dot_general(a, b, (((0,), (0,)), ((), ())), preferred_element_type=F32)


def norm(v):
    centred = v - jnp.mean(v, 0, keepdims=True)
    inverse = lax.rsqrt(jnp.mean(centred * centred, 0, keepdims=True) + EPSILON)
    return centred * inverse, inverse


def norm_back(h, hat, inverse):
    first = jnp.mean(h, 0, keepdims=True)
    second = jnp.mean(h * hat, 0, keepdims=True)
    return (h - first - hat * second) * inverse


def sigmoid(v):
    return 1.0 / (1.0 + jnp.exp(-v))


def pad_rows(v, rows):
    return jnp.concatenate([v, jnp.zeros((rows - v.shape[0],) + v.shape[1:], v.dtype)], 0)


def flip(v):
    return pad_rows(v, WIDE).T


def low_half(v):
    lane = lax.broadcasted_iota(jnp.int32, v.shape, v.ndim - 1)
    return jnp.where(lane < 64, v, 0.0)


def pack(a, b):
    tail = low_half(a[:, 128:]) + pltpu.roll(low_half(b[:, 128:]), 64, 1)
    return a[:, :128], b[:, :128], tail


def unpack(t0, t1, t2):
    return (t0, low_half(t2)), (t1, low_half(pltpu.roll(t2, 64, 1)))


def as_column(row_ref):
    n = row_ref.shape[1]
    a = lax.broadcasted_iota(jnp.int32, (n, n), 0)
    b = lax.broadcasted_iota(jnp.int32, (n, n), 1)
    return jnp.sum(jnp.where(a == b, row_ref[...], 0.0), 1, keepdims=True)


def as_row(column):
    n = column.shape[0]
    a = lax.broadcasted_iota(jnp.int32, (n, n), 0)
    b = lax.broadcasted_iota(jnp.int32, (n, n), 1)
    return jnp.sum(jnp.where(a == b, column, 0.0), 0, keepdims=True)


class Coming:
    def __init__(self, far, buffer, sems, axis):
        self.far, self.buffer, self.sems, self.axis = far, buffer, sems, axis
        self.shape, self.at = buffer.shape, buffer.at
        for k in range(sems.shape[0]):
            self.copy(k).start()

    def __getitem__(self, index):
        return self.buffer[index]

    def copy(self, k):
        size = self.shape[self.axis] // self.sems.shape[0]
        cut = (slice(None),) * self.axis + (pl.ds(k * size, size),)
        return pltpu.make_async_copy(self.far.at[cut], self.buffer.at[cut], self.sems.at[k])

    def wait(self, k=0):
        self.copy(k).wait()


def call(us, kernel, outs, scratch, *operands, smem=0, away=0, sems=None, far=None):
    far = far or {}
    operands = [
        pltpu.with_memory_space_constraint(v, pltpu.HBM) if i in far else v
        for i, v in enumerate(operands)
    ]
    specs = [pl.BlockSpec(memory_space=pltpu.SMEM)] * smem
    specs += [
        pl.BlockSpec(memory_space=pltpu.HBM if i in far else pltpu.VMEM)
        for i in range(smem, len(operands))
    ]
    room = [pltpu.VMEM(s, t) for s, t in scratch]
    if away:
        room.append(pltpu.SemaphoreType.DMA(sems or (away,)))
    plain = len(operands) + len(outs) + len(room)
    for i, (pieces, _) in far.items():
        room.append(pltpu.VMEM(operands[i].shape, operands[i].dtype))
        room.append(pltpu.SemaphoreType.DMA((pieces,)))

    def wrapped(*refs):
        refs = list(refs)
        for k, (i, (_, axis)) in enumerate(far.items()):
            refs[i] = Coming(refs[i], refs[plain + 2 * k], refs[plain + 2 * k + 1], axis)
        kernel(*refs[:plain])

    return pl.pallas_call(
        wrapped,
        out_shape=[
            pltpu.HBM(s, t) if math.prod(s) > 131072 else jax.ShapeDtypeStruct(s, t)
            for s, t in outs
        ],
        in_specs=specs,
        out_specs=[pl.BlockSpec(memory_space=pltpu.VMEM)] * (len(outs) - away)
        + [pl.BlockSpec(memory_space=pltpu.HBM)] * away,
        scratch_shapes=room,
        compiler_params=pltpu.CompilerParams(vmem_limit_bytes=50 * 1024 * 1024),
        cost_estimate=pl.CostEstimate(flops=us * 10**9, bytes_accessed=0, transcendentals=0),
    )(*operands)


def project_kernel(
    x_ref, gain_ref, w_ref, left_ref, rsend_out, lsend_out, rsend_ref, lsend_ref, sems
):
    pairs = x_ref.shape[0]
    width = w_ref.shape[0]
    half = w_ref.shape[1] // 2
    gain = as_column(gain_ref)

    @pl.loop(0, pairs, unroll=3)
    def _(m):
        x = flip(x_ref[m].astype(F32))
        both = []
        for o in range(2):
            hat, _ = norm(x[o * width : (o + 1) * width])
            proj = tn(w_ref[...], (hat * gain).astype(BF))
            both.append(proj)
            left_ref[2 * m + o] = proj[:half].astype(BF)
        for t, v in enumerate(pack(both[0][:half], both[1][:half])):
            lsend_ref[m, t] = v.astype(BF)
        for t, v in enumerate(pack(both[0][half:], both[1][half:])):
            rsend_ref[m, t] = v.astype(BF)

    copies = []
    for k in range(rsend_out.shape[0]):
        copies.append(pltpu.make_async_copy(rsend_ref, rsend_out.at[k], sems.at[0, k]))
        copies.append(pltpu.make_async_copy(lsend_ref, lsend_out.at[k], sems.at[1, k]))
    for c in copies:
        c.start()
    for c in copies:
        c.wait()


def load_wide(head, tail, start, count, stride):
    a = head[pl.ds(start, count, stride=stride), :]
    b = tail[pl.ds(start, count, stride=stride), :]
    return jnp.concatenate([a, b], 1)


def store_wide(head, tail, start, count, stride, v):
    head[pl.ds(start, count, stride=stride), :] = v[:, :128]
    tail[pl.ds(start, count, stride=stride), :] = v[:, 128:]


def spread_projections(source, first, step, pitch, head, tail):
    pairs, _, half, _ = source.shape
    for m in range(pairs):
        t = source[m].astype(F32)
        for o, (a, b) in enumerate(unpack(t[0], t[1], t[2])):
            at = pl.ds((first + step * (2 * m + o)) * pitch, half)
            head[at, :] = a
            tail[at, :] = b


def outer_kernel(
    par_ref, own_ref, other_ref, left_ref, edge_ref, wt_ref, bias_ref, gain_ref, entry_ref,
    send_ref, mid_ref, normed_ref, right_out, outer_out,
    head, tail, right_ref, outer_ref, sems,
):
    chips, pairs, _, half, _ = own_ref.shape
    rows = left_ref.shape[0]
    length = edge_ref.shape[1]
    depth = 1.0 / length
    pitch = half + 1
    par = par_ref[0]
    for source, p in ((own_ref, par), (other_ref, 1 - par)):
        source.wait()

        @pl.loop(0, chips, unroll=2)
        def _(chip):
            spread_projections(source.at[chip], (2 * chip + p) * rows, 1, pitch, head, tail)

    left = left_ref[...].reshape(rows * half, WIDE)

    @pl.loop(0, half, unroll=4)
    def _(q):
        r = pad_rows(load_wide(head, tail, q, length, pitch), WIDE).astype(BF)
        right_ref[q] = r
        o = (nt(left, r) * depth).astype(BF)
        at = pl.ds(pl.multiple_of(q * half, half), half)
        for i in range(rows):
            outer_ref[i, at, :] = o[i * half : (i + 1) * half]

    copies = [
        pltpu.make_async_copy(right_ref, right_out, sems.at[0]),
        pltpu.make_async_copy(outer_ref, outer_out, sems.at[1]),
    ]
    for c in copies:
        c.start()
    devices, _, _, sixteen, _ = send_ref.shape
    bias = as_column(bias_ref)
    gain = as_column(gain_ref)
    for ref in (edge_ref, wt_ref, entry_ref):
        ref.wait()

    @pl.loop(0, pairs, unroll=3)
    def _(m):
        both = []
        for o in range(2):
            i = 2 * m + o
            mid = flip(edge_ref[i].astype(F32)) + (nn(wt_ref[...], outer_ref[i]) + bias)
            mid_ref[i] = mid
            hat, _ = norm(mid)
            normed = (hat * gain).astype(BF)
            normed_ref[i] = normed
            raw = nn(entry_ref[...], normed)
            cut = raw.shape[0] // 2
            both.append(sigmoid(raw[:cut]) * raw[cut:])
        for t, v in enumerate(pack(*both)):
            send_ref[:, m, t] = v.reshape(devices, sixteen, 128).astype(BF)

    for c in copies:
        c.wait()


def gate_kernel(normed_ref, adj_ref, wg_ref, gate_ref, up_ref):
    @pl.loop(0, normed_ref.shape[0])
    def _(i):
        gate_ref[i] = sigmoid(tn(wg_ref[...], normed_ref[i]))
        up_ref[i] = flip(adj_ref[i].astype(F32)).astype(BF)


def spread(source, half, head, tail):
    devices, pairs, _, high, _ = source.shape
    many = high // half

    @pl.loop(0, devices, unroll=4)
    def _(d):
        for m in range(pairs):
            t = source[d, m].astype(F32)
            for o, (a, b) in enumerate(unpack(t[0], t[1], t[2])):
                for g in range(many):
                    at = pl.ds((((d * pairs + m) * 2 + o) * many + g) * (half + 1), half)
                    head[at, :] = a[g * half : (g + 1) * half]
                    tail[at, :] = b[g * half : (g + 1) * half]


def gather_up(half, head, tail, target):
    devices, pairs, _, high, _ = target.shape
    many = high // half

    @pl.loop(0, devices, unroll=4)
    def _(d):
        for m in range(pairs):
            wide = []
            for o in range(2):
                got = []
                for g in range(many):
                    at = pl.ds((((d * pairs + m) * 2 + o) * many + g) * (half + 1), half)
                    got.append(jnp.concatenate([head[at, :], tail[at, :]], 1))
                wide.append(jnp.concatenate(got, 0))
            for t, v in enumerate(pack(*wide)):
                target[d, m, t] = v.astype(BF)


def triangle_kernel(
    edges_ref, send_ref, left_out, right_out, head, tail, mhead, mtail, left_ref, right_ref, sems
):
    channels, length, _ = left_ref.shape
    spread(edges_ref, 2 * channels, head, tail)
    for c in range(channels):
        a = load_wide(head, tail, c, length, 2 * channels + 1).astype(BF)
        b = load_wide(head, tail, channels + c, length, 2 * channels + 1).astype(BF)
        left_ref[c] = a
        right_ref[c] = b
        mixed = tn(a, b)[:length]
        store_wide(mhead, mtail, c, length, channels + 1, mixed)
    copies = [
        pltpu.make_async_copy(left_ref, left_out, sems.at[0]),
        pltpu.make_async_copy(right_ref, right_out, sems.at[1]),
    ]
    for c in copies:
        c.start()
    gather_up(channels, mhead, mtail, send_ref)
    for c in copies:
        c.wait()


def triangle_back_kernel(grads_ref, left_ref, right_ref, send_ref, head, tail, mhead, mtail):
    channels, length, _ = left_ref.shape
    spread(grads_ref, channels, mhead, mtail)
    left_ref.wait()
    right_ref.wait()
    for c in range(channels):
        g = pad_rows(load_wide(mhead, mtail, c, length, channels + 1), WIDE).astype(BF)
        store_wide(head, tail, c, length, 2 * channels + 1, nt(right_ref[c], g))
        store_wide(head, tail, channels + c, length, 2 * channels + 1, nn(left_ref[c], g))
    gather_up(2 * channels, head, tail, send_ref)


def mixed_rows(mixed_ref, n):
    devices, _, _, sixteen, _ = mixed_ref.shape
    eight = sixteen // 2
    t = [mixed_ref[:, n, k].astype(F32).reshape(devices * sixteen, 128) for k in range(3)]
    out = []
    for a, b in unpack(*t):
        block = jnp.concatenate([a, b], 1).reshape(devices, 2, eight, WIDE)
        out += [block[:, o].reshape(devices * eight, WIDE) for o in range(2)]
    return out


def update_kernel(mixed_ref, gate_ref, up_ref, cgain_ref, wf_ref, send_ref):
    devices, quads, _, sixteen, _ = mixed_ref.shape
    cgain = as_column(cgain_ref)

    @pl.loop(0, quads, unroll=3)
    def _(n):
        grads = []
        for k, mixed in enumerate(mixed_rows(mixed_ref, n)):
            i = 4 * n + k
            hat, inverse = norm(mixed)
            gu = (up_ref[i].astype(F32) * gate_ref[i]).astype(BF)
            gmn = nn(wf_ref[...], gu)
            back = norm_back(gmn * cgain, hat, inverse)
            grads.append(back.reshape(devices, 1, sixteen // 2, WIDE))
        packed = [
            jnp.concatenate(grads[2 * o : 2 * o + 2], 1).reshape(devices * sixteen, WIDE)
            for o in range(2)
        ]
        for k, v in enumerate(pack(*packed)):
            send_ref[:, n, k] = v.reshape(devices, sixteen, 128).astype(BF)


def result_kernel(
    mixed_ref, mid_ref, normed_ref, gate_ref, up_ref, cgain_ref, wf_ref,
    out_ref, ggate_ref, wfg_ref, wgg_ref, msum_ref, acc,
):
    _, quads, _, _, _ = mixed_ref.shape
    length = out_ref.shape[1]
    wfg_ref[...] = jnp.zeros_like(wfg_ref)
    wgg_ref[...] = jnp.zeros_like(wgg_ref)
    acc[...] = jnp.zeros_like(acc)
    cgain = as_column(cgain_ref)
    for ref in (mixed_ref, mid_ref, normed_ref, gate_ref, up_ref):
        ref.wait()

    @pl.loop(0, quads)
    def _(n):
        for k, mixed in enumerate(mixed_rows(mixed_ref, n)):
            i = 4 * n + k
            hat, _ = norm(mixed)
            mn = (hat * cgain).astype(BF)
            gate = gate_ref[i]
            update = tn(wf_ref[...], mn)
            new = mid_ref[i] + gate * update
            out_ref[i] = new.T[:length].astype(BF)
            upgate = up_ref[i].astype(F32) * gate
            gu = upgate.astype(BF)
            gg = (upgate * update * (1.0 - gate)).astype(BF)
            ggate_ref[i] = gg
            wfg_ref[...] += nt(mn, gu)
            wgg_ref[...] += nt(normed_ref[i], gg)
            acc[...] += nn(wf_ref[...], gu) * hat

    msum_ref[...] = jnp.sum(acc[...].T, 0, keepdims=True)


def edge_back_kernel(
    grads_ref, mid_ref, normed_ref, ggate_ref, up_ref, gain_ref, entryt_ref, entry_ref, wg_ref,
    pgrad_ref, pgradt_ref, send_ref, win_ref, gsum_ref, bsum_ref, gacc, bacc, rows,
):
    devices, pairs, _, sixteen, _ = grads_ref.shape
    count, length, channels = pgrad_ref.shape
    win_ref[...] = jnp.zeros_like(win_ref)
    gacc[...] = jnp.zeros_like(gacc)
    bacc[...] = jnp.zeros_like(bacc)
    gain = as_column(gain_ref)

    def step(m):
        t = [grads_ref[:, m, k].astype(F32).reshape(devices * sixteen, 128) for k in range(3)]
        for o, (a, b) in enumerate(unpack(*t)):
            i = 2 * m + o
            grad = jnp.concatenate([a, b], 1)
            normed = normed_ref[i]
            raw = nn(entryt_ref[...], normed)
            cut = raw.shape[0] // 2
            sig = sigmoid(raw[:cut])
            gs = grad * sig
            graw = jnp.concatenate([gs * raw[cut:] * (1.0 - sig), gs], 0).astype(BF)
            win_ref[...] += nt(graw, normed)
            gpn = nn(entry_ref[...], graw) + nn(wg_ref[...], ggate_ref[i])
            hat, inverse = norm(mid_ref[i])
            gacc[...] += gpn * hat
            gmid = up_ref[i].astype(F32) + norm_back(gpn * gain, hat, inverse)
            bacc[...] += gmid
            pgradt_ref[i] = gmid.astype(BF)
            turned = gmid.T[:length]
            pgrad_ref[i] = turned.astype(BF)
            rows[pl.ds(i, length, stride=count), :] = turned

    third = pairs // 2
    for h in range(2):
        for ref in (grads_ref, mid_ref, normed_ref, ggate_ref, up_ref):
            ref.wait(h)
        pl.loop(h * third, (h + 1) * third, unroll=third)(step)

    send_ref[...] = rows[...].astype(BF)
    gsum_ref[...] = jnp.sum(gacc[...].T, 0, keepdims=True)
    bsum_ref[...] = jnp.sum(bacc[...].T, 0, keepdims=True)


def prepare_kernel(par_ref, own_ref, other_ref, x_ref, left_ref, hat_ref, inv_ref, head, tail):
    chips, pairs, _, half, _ = own_ref.shape
    length = left_ref.shape[1] * 3 // 4
    devices = 2 * chips
    pitch = half + 1
    par = par_ref[0]
    for source, p in ((own_ref, par), (other_ref, 1 - par)):

        @pl.loop(0, chips)
        def _(chip):
            spread_projections(source.at[chip], 2 * chip + p, devices, pitch, head, tail)

    @pl.loop(0, half, unroll=2)
    def _(q):
        left_ref[q] = pad_rows(load_wide(head, tail, q, length, pitch), WIDE).astype(BF)

    width = hat_ref.shape[1]

    @pl.loop(0, pairs)
    def _(m):
        x = flip(x_ref[m].astype(F32))
        for o in range(2):
            hat, inverse = norm(x[o * width : (o + 1) * width])
            hat_ref[2 * m + o] = hat
            inv_ref[2 * m + o] = inverse


def put(stage, i, g):
    half = g.shape[0] // (stage.shape[0] * (stage.shape[2] // WIDE))
    group = stage.shape[2] // WIDE
    at = pl.ds(pl.multiple_of(i * half, half), half)
    for q in range(g.shape[0] // half):
        lanes = slice((q % group) * WIDE, (q % group + 1) * WIDE)
        stage[q // group, at, lanes] = g[q * half : (q + 1) * half]


def contract(stage, projections, total):
    group = stage.shape[2] // WIDE
    total[...] = jnp.zeros_like(total)

    @pl.loop(0, stage.shape[0], unroll=4)
    def _(k):
        r = projections[pl.ds(k * group, group)].reshape(group * WIDE, WIDE)
        total[...] += nn(stage[k], r)


def weight_kernel(
    pgradt_ref, outer_ref, win_ref, wgg_ref, wfg_ref, cgain_ref, pgain_ref, bias_ref,
    out_ref, wacc, wout,
):
    count = pgradt_ref.shape[0]
    many = wacc.shape[0]
    half = out_ref.shape[1] // 4
    wacc[...] = jnp.zeros_like(wacc)

    def step(m):
        a = jnp.concatenate([outer_ref[2 * m], outer_ref[2 * m + 1]], 1)
        b = jnp.concatenate([pgradt_ref[2 * m], pgradt_ref[2 * m + 1]], 1)
        wacc[...] += nt(a, b)

    third = count // 4
    for h in range(2):
        outer_ref.wait(h)
        pl.loop(h * third, (h + 1) * third, unroll=third)(step)

    for q in range(half):
        wout[pl.ds(q, half, stride=half + 1), :] = wacc[q * half : (q + 1) * half, :]
    for p in range(half):
        out_ref[p * half : (p + 1) * half, :] = wout[
            p * (half + 1) : p * (half + 1) + half, :
        ].astype(BF)
    at = many
    for ref in (win_ref, wgg_ref, wfg_ref):
        out_ref[at : at + ref.shape[0], :] = ref[...].astype(BF)
        at += ref.shape[0]
    rest = [cgain_ref[...], pgain_ref[...], bias_ref[...], jnp.zeros((13, 128), F32)]
    out_ref[at : at + 16, :] = jnp.concatenate(rest, 0).astype(BF)
    at += 16
    out_ref[at:, :] = jnp.zeros((out_ref.shape[0] - at, 128), BF)


def outer_back_kernel(pgradt_ref, right_ref, w_ref, grad_ref, stage):
    count, _, _ = pgradt_ref.shape
    depth = 1.0 / (right_ref.shape[1] * 3 // 4)

    @pl.loop(0, count, unroll=4)
    def _(i):
        put(stage, i, nn(w_ref[...], pgradt_ref[i]).astype(BF))

    right_ref.wait()
    contract(stage, right_ref, grad_ref)
    grad_ref[...] = grad_ref[...] * depth


def column_kernel(
    pcol_ref, left_ref, w_ref, gleft_ref, hat_ref, inv_ref, mgain_ref, wmap_ref,
    out_ref, cross_ref, prow, stage, gright, cacc,
):
    devices, many, channels = pcol_ref.shape
    half = left_ref.shape[0]
    count = gleft_ref.shape[0] // half
    length = devices * count
    pairs = count // 2

    @pl.loop(0, devices, unroll=4)
    def _(d):
        prow[pl.ds(d * (many + 1), many), :] = pcol_ref[d].astype(F32)

    @pl.loop(0, count, unroll=4)
    def _(j):
        p = jnp.concatenate(
            [prow[pl.ds(j * count + i, devices, stride=many + 1), :] for i in range(count)], 0
        )
        put(stage, j, nt(w_ref[...], pad_rows(p, WIDE).astype(BF)).astype(BF))

    left_ref.wait()
    contract(stage, left_ref, gright)
    gleft_ref.wait()
    hat_ref.wait()
    gain = as_column(mgain_ref)
    cacc[...] = jnp.zeros_like(cacc)

    @pl.loop(0, pairs, unroll=3)
    def _(m):
        both = []
        for o in range(2):
            i = 2 * m + o
            hat = hat_ref[i]
            at = pl.ds(pl.multiple_of(i * half, half), half)
            right = (gright[at, :] * (1.0 / length)).astype(BF)
            g = jnp.concatenate([gleft_ref[at, :].astype(BF), right], 0)
            cacc[...] += nt(hat.astype(BF), pad_rows(g, 128))
            both.append(norm_back(nn(wmap_ref[...], g) * gain, hat, inv_ref[i]))
        out_ref[m] = jnp.concatenate(both, 0).T[:length].astype(BF)

    rows = cross_ref.shape[0]
    cross_ref[...] = (cacc[:rows, :] + pltpu.roll(cacc[rows:, :], 64, 1)).astype(BF)


def finish_kernel(
    factor, all_ref, gain_ref, wmap_ref,
    mgain_out, proj_out, wout_out, bias_out, pgain_out, win_out, wgg_out, cgain_out, wfg_out,
    rows, flat,
):
    everyone, each, _ = all_ref.shape
    width = proj_out.shape[0]
    own = each - width // 2
    eight = 8

    @pl.loop(0, everyone)
    def _(d):
        rows[pl.ds(pl.multiple_of(d * own, 16), own), :] = all_ref[d, :own].astype(F32) * factor

    many = wout_out.shape[0]
    wout_out[...] = rows[:many, :]
    at = many
    channels = wgg_out.shape[0]
    devices = channels // eight
    for k in range(4):
        lr, gv = k // 2, k % 2
        for d in range(devices):
            start = at + gv * 2 * channels + d * 2 * eight + lr * eight
            flat[d * eight : (d + 1) * eight, :] = rows[start : start + eight, :]
        win_out[:, k * channels : (k + 1) * channels] = flat[...].T
    at += 4 * channels
    wgg_out[...] = rows[at : at + channels, :]
    at += channels
    wfg_out[...] = rows[at : at + channels, :]
    at += channels
    cgain_out[...] = rows[at : at + 1, :]
    pgain_out[...] = rows[at + 1 : at + 2, :]
    bias_out[...] = rows[at + 2 : at + 3, :]
    cross = jnp.sum(all_ref[:, own:].astype(F32), 0) * factor
    cross = jnp.concatenate([cross, pltpu.roll(cross, 64, 1)], 0)[:, :width]
    proj_out[...] = cross * as_column(gain_ref)
    mgain_out[...] = as_row(jnp.sum(cross * wmap_ref[...].astype(F32), 1, keepdims=True))


def exchange(v, axes="dap", groups=None):
    return lax.all_to_all(
        v, axes, split_axis=0, concat_axis=0, tiled=True, axis_index_groups=groups
    )


def local(
    homolog_features,
    edge_features,
    adjoint_edges,
    homolog_scaling_factor,
    tensor_mapping_matrix,
    tensor_final_matrix,
    tensor_final_offset,
    edge_scaling_factor,
    trilateral_entry_matrix,
    final_sigmoid_matrix,
    central_scaling_factor,
    trilateral_final_matrix,
):
    n = lax.axis_size("dap")
    msa = homolog_features[0]
    depth, count, width = msa.shape
    length = edge_features.shape[2]
    pairs = count // 2
    half = tensor_mapping_matrix.shape[1] // 2
    channels = edge_features.shape[3]
    eight = channels // n
    edges = edge_features[0]
    adjoint = adjoint_edges[0]
    line = lambda v: v.reshape(1, -1)
    msa_gain = line(homolog_scaling_factor)

    x = msa.reshape(depth, pairs, 2 * width).transpose(1, 0, 2)
    chips = n // 2
    left, right_send, left_send = call(
        2,
        project_kernel,
        [((count, half, WIDE), BF)] + [((chips, pairs, 3, half, 128), BF)] * 2,
        [((pairs, 3, half, 128), BF)] * 2,
        x, msa_gain, tensor_mapping_matrix,
        away=2, sems=(2, chips),
    )
    groups = [list(range(0, n, 2)), list(range(1, n, 2))]

    def sibling(v):
        return lax.ppermute(v, "dap", [(i, i ^ 1) for i in range(n)])

    own = exchange(right_send, groups=groups)
    other = sibling(own)
    left_send, other = lax.optimization_barrier((left_send, other))
    left_own = exchange(left_send, groups=groups)
    parity = lax.rem(lax.axis_index("dap"), 2).astype(jnp.int32).reshape(1)

    qp = tensor_final_matrix.reshape(half, half, channels).transpose(1, 0, 2)
    qp = qp.reshape(half * half, channels)
    entry = trilateral_entry_matrix.reshape(channels, 2, 2, n, eight).transpose(0, 2, 3, 1, 4)
    entry = entry.reshape(channels, 4 * channels)
    wide = ((count, channels, WIDE), BF)
    wide32 = ((count, channels, WIDE), F32)
    every = ((half, WIDE, WIDE), BF)
    outers = ((count, half * half, WIDE), BF)
    spare = [((length * (half + 1), 128), F32)] * 2
    edge_send, mid, normed, right, outer = call(
        14,
        outer_kernel,
        [((n, pairs, 3, 2 * eight, 128), BF), wide32, wide, every, outers],
        spare + [every, outers],
        parity, own, other, left, edges, qp.T, line(tensor_final_offset),
        line(edge_scaling_factor), entry.T, smem=1, away=2,
        far={1: (1, 0), 2: (1, 0), 4: (1, 0), 5: (1, 0), 8: (1, 0)},
    )
    edge_send, left_own = lax.optimization_barrier((edge_send, left_own))
    edge_cols = exchange(edge_send)
    left_other = sibling(left_own)
    gate, up = call(3, gate_kernel, [wide32, wide], [], normed, adjoint, final_sigmoid_matrix)
    rooms = [((length * (2 * eight + 1), 128), F32)] * 2
    rooms += [((length * (eight + 1), 128), F32)] * 2
    mixed_send, left_cols, right_cols = call(
        3,
        triangle_kernel,
        [((n, pairs // 2, 3, 2 * eight, 128), BF)] + [((eight, length, WIDE), BF)] * 2,
        rooms + [((eight, length, WIDE), BF)] * 2,
        edge_cols,
        away=2,
    )
    mixed_send, gate, up = lax.optimization_barrier((mixed_send, gate, up))
    mixed = exchange(mixed_send)
    square = ((channels, channels), F32)
    row = ((1, channels), F32)
    (grad_send,) = call(
        2,
        update_kernel,
        [((n, pairs // 2, 3, 2 * eight, 128), BF)],
        [],
        mixed, gate, up, line(central_scaling_factor), trilateral_final_matrix,
    )
    grad_cols = exchange(grad_send)
    pair_out, grad_gate, tri_out, tri_gate, mid_gain = call(
        6,
        result_kernel,
        [(edges.shape, BF), wide, square, square, row],
        [((channels, WIDE), F32)],
        mixed, mid, normed, gate, up, line(central_scaling_factor), trilateral_final_matrix,
        far={i: (1, 0) for i in range(5)},
    )
    (back_send,) = call(
        4,
        triangle_back_kernel,
        [((n, pairs, 3, 2 * eight, 128), BF)],
        rooms,
        grad_cols, left_cols, right_cols,
        far={1: (1, 0), 2: (1, 0)},
    )
    back = exchange(back_send)
    left_own, left_other, back_send = lax.optimization_barrier((left_own, left_other, back_send))
    lefts, hat, inverse = call(
        6,
        prepare_kernel,
        [every, ((count, width, WIDE), F32), ((count, 1, WIDE), F32)],
        spare,
        parity, left_own, left_other, x, smem=1,
    )
    pgrad, pgradt, pgrad_send, tri_in, tri_gain, bias = call(
        9,
        edge_back_kernel,
        [
            (edges.shape, BF), wide, ((length * count, channels), BF),
            ((4 * channels, channels), F32), row, row,
        ],
        [((channels, WIDE), F32)] * 2 + [((length * count, channels), F32)],
        back, mid, normed, grad_gate, up, line(edge_scaling_factor),
        entry.T, entry, final_sigmoid_matrix,
        far={0: (2, 1), 1: (2, 0), 2: (2, 0), 3: (2, 0), 4: (2, 0)},
    )
    pgrad_cols = exchange(pgrad_send.reshape(n, count * count, channels))
    group = 4
    stage = ((half // group, count * half, group * WIDE), BF)
    grads = ((count * half, WIDE), F32)
    cross = ((width // 2, 128), BF)
    full = ((half * half, channels), F32)
    used = half * half + 6 * channels + 3
    each = -(-used // (16 * n)) * 16
    (weights,) = call(
        6,
        weight_kernel,
        [((each * n, channels), BF)],
        [full, ((half * (half + 1), channels), F32)],
        pgradt, outer, tri_in, tri_gate, tri_out, mid_gain, tri_gain, bias,
        far={1: (2, 0)},
    )
    (grad_left,) = call(
        7, outer_back_kernel, [grads], [stage], pgradt, right, qp, far={1: (1, 0)}
    )
    weights, pgrad_cols = lax.optimization_barrier((weights, pgrad_cols))
    mine = exchange(weights.reshape(n, each, channels))
    sens, cross = call(
        9,
        column_kernel,
        [((pairs, length, 2 * width), BF), cross],
        [((devices_rows(n, count), channels), F32), stage, grads, ((width, 128), F32)],
        pgrad_cols, lefts, tensor_final_matrix, grad_left, hat, inverse,
        msa_gain, tensor_mapping_matrix,
        far={1: (1, 0), 3: (1, 0), 4: (1, 0)},
    )
    sensitivity = sens.transpose(1, 0, 2).reshape(depth, count, width)
    crops = lax.axis_size("dp")
    mine = jnp.concatenate([jnp.sum(mine.astype(F32), 0).astype(BF), cross], 0)
    mine = exchange(jnp.broadcast_to(mine, (crops,) + mine.shape), "dp")
    mine = jnp.sum(mine.astype(F32), 0).astype(BF)
    total = exchange(jnp.broadcast_to(mine, (n,) + mine.shape))
    factor = 1.0 / (crops * length)
    last = call(
        2,
        lambda *refs: finish_kernel(factor, *refs),
        [
            ((1, width), F32), ((width, 2 * half), F32), full, row, row,
            ((channels, 4 * channels), F32), square, row, square,
        ],
        [((n * each, 128), F32), ((channels, 128), F32)],
        total, msa_gain, tensor_mapping_matrix,
    )
    last = [v.reshape(-1) if v.shape[0] == 1 else v for v in last]
    return (pair_out[None], pgrad[None], sensitivity[None], *last)


def devices_rows(devices, count):
    return devices * (count * count + 1)


def solution(mesh):
    placed = (
        P("dp", None, "dap", None),
        P("dp", "dap", None, None),
        P("dp", "dap", None, None),
    ) + (P(),) * 9
    return jax.shard_map(
        local,
        mesh=mesh,
        in_specs=placed,
        out_specs=(
            P("dp", "dap", None, None),
            P("dp", "dap", None, None),
            P("dp", None, "dap", None),
        )
        + (P(),) * 9,
        check_vma=False,
    )
```

```python
import math

import jax
import jax.numpy as jnp
from jax import lax
from jax.experimental import pallas as pl
from jax.experimental.pallas import tpu as pltpu
from jax.sharding import PartitionSpec as P

EPSILON = 1e-05
BF = jnp.bfloat16
F32 = jnp.float32
WIDE = 256


def nn(a, b):
    return lax.dot_general(a, b, (((1,), (0,)), ((), ())), preferred_element_type=F32)


def nt(a, b):
    return lax.dot_general(a, b, (((1,), (1,)), ((), ())), preferred_element_type=F32)


def tn(a, b):
    return lax.dot_general(a, b, (((0,), (0,)), ((), ())), preferred_element_type=F32)


def norm(v):
    centred = v - jnp.mean(v, 0, keepdims=True)
    inverse = lax.rsqrt(jnp.mean(centred * centred, 0, keepdims=True) + EPSILON)
    return centred * inverse, inverse


def norm_back(h, hat, inverse):
    first = jnp.mean(h, 0, keepdims=True)
    second = jnp.mean(h * hat, 0, keepdims=True)
    return (h - first - hat * second) * inverse


def sigmoid(v):
    return 1.0 / (1.0 + jnp.exp(-v))


def pad_rows(v, rows):
    return jnp.concatenate([v, jnp.zeros((rows - v.shape[0],) + v.shape[1:], v.dtype)], 0)


def flip(v):
    return pad_rows(v, WIDE).T


def low_half(v):
    lane = lax.broadcasted_iota(jnp.int32, v.shape, v.ndim - 1)
    return jnp.where(lane < 64, v, 0.0)


def pack(a, b):
    tail = low_half(a[:, 128:]) + pltpu.roll(low_half(b[:, 128:]), 64, 1)
    return a[:, :128], b[:, :128], tail


def unpack(t0, t1, t2):
    return (t0, low_half(t2)), (t1, low_half(pltpu.roll(t2, 64, 1)))


def as_column(row_ref):
    n = row_ref.shape[1]
    a = lax.broadcasted_iota(jnp.int32, (n, n), 0)
    b = lax.broadcasted_iota(jnp.int32, (n, n), 1)
    return jnp.sum(jnp.where(a == b, row_ref[...], 0.0), 1, keepdims=True)


def as_row(column):
    n = column.shape[0]
    a = lax.broadcasted_iota(jnp.int32, (n, n), 0)
    b = lax.broadcasted_iota(jnp.int32, (n, n), 1)
    return jnp.sum(jnp.where(a == b, column, 0.0), 0, keepdims=True)


class Coming:
    def __init__(self, far, buffer, sems, axis):
        self.far, self.buffer, self.sems, self.axis = far, buffer, sems, axis
        self.shape, self.at = buffer.shape, buffer.at

    def __getitem__(self, index):
        return self.buffer[index]

    def copy(self, k):
        size = self.shape[self.axis] // self.sems.shape[0]
        cut = (slice(None),) * self.axis + (pl.ds(k * size, size),)
        return pltpu.make_async_copy(self.far.at[cut], self.buffer.at[cut], self.sems.at[k])

    def wait(self, k=0):
        self.copy(k).wait()


def call(us, kernel, outs, scratch, *operands, smem=0, away=0, sems=None, far=None):
    far = far or {}
    operands = [
        pltpu.with_memory_space_constraint(v, pltpu.HBM) if i in far else v
        for i, v in enumerate(operands)
    ]
    specs = [pl.BlockSpec(memory_space=pltpu.SMEM)] * smem
    specs += [
        pl.BlockSpec(memory_space=pltpu.HBM if i in far else pltpu.VMEM)
        for i in range(smem, len(operands))
    ]
    room = [pltpu.VMEM(s, t) for s, t in scratch]
    if away:
        room.append(pltpu.SemaphoreType.DMA(sems or (away,)))
    plain = len(operands) + len(outs) + len(room)
    for i, (pieces, _) in far.items():
        room.append(pltpu.VMEM(operands[i].shape, operands[i].dtype))
        room.append(pltpu.SemaphoreType.DMA((pieces,)))

    def wrapped(*refs):
        refs = list(refs)
        for k, (i, (_, axis)) in enumerate(far.items()):
            refs[i] = Coming(refs[i], refs[plain + 2 * k], refs[plain + 2 * k + 1], axis)
        for k in range(max([pieces for pieces, _ in far.values()], default=0)):
            for i, (pieces, _) in far.items():
                if k < pieces:
                    refs[i].copy(k).start()
        kernel(*refs[:plain])

    return pl.pallas_call(
        wrapped,
        out_shape=[
            pltpu.HBM(s, t) if math.prod(s) > 131072 else jax.ShapeDtypeStruct(s, t)
            for s, t in outs
        ],
        in_specs=specs,
        out_specs=[pl.BlockSpec(memory_space=pltpu.VMEM)] * (len(outs) - away)
        + [pl.BlockSpec(memory_space=pltpu.HBM)] * away,
        scratch_shapes=room,
        compiler_params=pltpu.CompilerParams(vmem_limit_bytes=50 * 1024 * 1024),
        cost_estimate=pl.CostEstimate(flops=us * 10**9, bytes_accessed=0, transcendentals=0),
    )(*operands)


def project_kernel(
    x_ref, gain_ref, w_ref, left_ref, rsend_out, lsend_out, rsend_ref, lsend_ref, sems
):
    pairs = x_ref.shape[0]
    width = w_ref.shape[0]
    half = w_ref.shape[1] // 2
    gain = as_column(gain_ref)

    @pl.loop(0, pairs, unroll=3)
    def _(m):
        x = flip(x_ref[m].astype(F32))
        both = []
        for o in range(2):
            hat, _ = norm(x[o * width : (o + 1) * width])
            proj = tn(w_ref[...], (hat * gain).astype(BF))
            both.append(proj)
            left_ref[2 * m + o] = proj[:half].astype(BF)
        for t, v in enumerate(pack(both[0][:half], both[1][:half])):
            lsend_ref[m, t] = v.astype(BF)
        for t, v in enumerate(pack(both[0][half:], both[1][half:])):
            rsend_ref[m, t] = v.astype(BF)

    copies = []
    for k in range(rsend_out.shape[0]):
        copies.append(pltpu.make_async_copy(rsend_ref, rsend_out.at[k], sems.at[0, k]))
        copies.append(pltpu.make_async_copy(lsend_ref, lsend_out.at[k], sems.at[1, k]))
    for c in copies:
        c.start()
    for c in copies:
        c.wait()


def load_wide(head, tail, start, count, stride):
    a = head[pl.ds(start, count, stride=stride), :]
    b = tail[pl.ds(start, count, stride=stride), :]
    return jnp.concatenate([a, b], 1)


def store_wide(head, tail, start, count, stride, v):
    head[pl.ds(start, count, stride=stride), :] = v[:, :128]
    tail[pl.ds(start, count, stride=stride), :] = v[:, 128:]


def spread_projections(source, first, step, pitch, head, tail):
    pairs, _, half, _ = source.shape
    for m in range(pairs):
        t = source[m].astype(F32)
        for o, (a, b) in enumerate(unpack(t[0], t[1], t[2])):
            at = pl.ds((first + step * (2 * m + o)) * pitch, half)
            head[at, :] = a
            tail[at, :] = b


def outer_kernel(
    par_ref, own_ref, other_ref, left_ref, edge_ref, wt_ref, bias_ref, gain_ref, entry_ref,
    send_ref, mid_ref, normed_ref, sig_ref, slope_ref, right_out, outer_out,
    head, tail, right_ref, outer_ref, sems,
):
    chips, pairs, _, half, _ = own_ref.shape
    rows = left_ref.shape[0]
    length = edge_ref.shape[1]
    depth = 1.0 / length
    pitch = half + 1
    par = par_ref[0]
    for source, p in ((own_ref, par), (other_ref, 1 - par)):
        source.wait()

        @pl.loop(0, chips, unroll=2)
        def _(chip):
            spread_projections(source.at[chip], (2 * chip + p) * rows, 1, pitch, head, tail)

    left = left_ref[...].reshape(rows * half, WIDE)

    @pl.loop(0, half, unroll=4)
    def _(q):
        r = pad_rows(load_wide(head, tail, q, length, pitch), WIDE).astype(BF)
        right_ref[q] = r
        o = (nt(left, r) * depth).astype(BF)
        at = pl.ds(pl.multiple_of(q * half, half), half)
        for i in range(rows):
            outer_ref[i, at, :] = o[i * half : (i + 1) * half]

    copies = [
        pltpu.make_async_copy(right_ref, right_out, sems.at[0]),
        pltpu.make_async_copy(outer_ref, outer_out, sems.at[1]),
    ]
    for c in copies:
        c.start()
    devices, _, _, sixteen, _ = send_ref.shape
    bias = as_column(bias_ref)
    gain = as_column(gain_ref)
    for ref in (edge_ref, wt_ref, entry_ref):
        ref.wait()

    @pl.loop(0, pairs, unroll=3)
    def _(m):
        both = []
        for o in range(2):
            i = 2 * m + o
            mid = flip(edge_ref[i].astype(F32)) + (nn(wt_ref[...], outer_ref[i]) + bias)
            mid_ref[i] = mid
            hat, _ = norm(mid)
            normed = (hat * gain).astype(BF)
            normed_ref[i] = normed
            raw = nn(entry_ref[...], normed)
            cut = raw.shape[0] // 2
            sig = sigmoid(raw[:cut])
            edge = sig * raw[cut:]
            both.append(edge)
            sig_ref[i] = sig.astype(BF)
            slope_ref[i] = (edge * (1.0 - sig)).astype(BF)
        for t, v in enumerate(pack(*both)):
            send_ref[:, m, t] = v.reshape(devices, sixteen, 128).astype(BF)

    for c in copies:
        c.wait()


def gate_kernel(normed_ref, adj_ref, wg_ref, gate_ref, up_ref):
    @pl.loop(0, normed_ref.shape[0])
    def _(i):
        gate_ref[i] = sigmoid(tn(wg_ref[...], normed_ref[i]))
        up_ref[i] = flip(adj_ref[i].astype(F32)).astype(BF)


def spread(source, half, head, tail):
    devices, pairs, _, high, _ = source.shape
    many = high // half

    @pl.loop(0, devices, unroll=4)
    def _(d):
        for m in range(pairs):
            t = source[d, m].astype(F32)
            for o, (a, b) in enumerate(unpack(t[0], t[1], t[2])):
                for g in range(many):
                    at = pl.ds((((d * pairs + m) * 2 + o) * many + g) * (half + 1), half)
                    head[at, :] = a[g * half : (g + 1) * half]
                    tail[at, :] = b[g * half : (g + 1) * half]


def gather_up(half, head, tail, target):
    devices, pairs, _, high, _ = target.shape
    many = high // half

    @pl.loop(0, devices, unroll=4)
    def _(d):
        for m in range(pairs):
            wide = []
            for o in range(2):
                got = []
                for g in range(many):
                    at = pl.ds((((d * pairs + m) * 2 + o) * many + g) * (half + 1), half)
                    got.append(jnp.concatenate([head[at, :], tail[at, :]], 1))
                wide.append(jnp.concatenate(got, 0))
            for t, v in enumerate(pack(*wide)):
                target[d, m, t] = v.astype(BF)


def triangle_kernel(
    edges_ref, send_ref, left_out, right_out, head, tail, mhead, mtail, left_ref, right_ref, sems
):
    channels, length, _ = left_ref.shape
    spread(edges_ref, 2 * channels, head, tail)
    for c in range(channels):
        a = load_wide(head, tail, c, length, 2 * channels + 1).astype(BF)
        b = load_wide(head, tail, channels + c, length, 2 * channels + 1).astype(BF)
        left_ref[c] = a
        right_ref[c] = b
        mixed = tn(a, b)[:length]
        store_wide(mhead, mtail, c, length, channels + 1, mixed)
    copies = [
        pltpu.make_async_copy(left_ref, left_out, sems.at[0]),
        pltpu.make_async_copy(right_ref, right_out, sems.at[1]),
    ]
    for c in copies:
        c.start()
    gather_up(channels, mhead, mtail, send_ref)
    for c in copies:
        c.wait()


def triangle_back_kernel(grads_ref, left_ref, right_ref, send_ref, head, tail, mhead, mtail):
    channels, length, _ = left_ref.shape
    spread(grads_ref, channels, mhead, mtail)
    left_ref.wait()
    right_ref.wait()
    for c in range(channels):
        g = pad_rows(load_wide(mhead, mtail, c, length, channels + 1), WIDE).astype(BF)
        store_wide(head, tail, c, length, 2 * channels + 1, nt(right_ref[c], g))
        store_wide(head, tail, channels + c, length, 2 * channels + 1, nn(left_ref[c], g))
    gather_up(2 * channels, head, tail, send_ref)


def mixed_rows(mixed_ref, n):
    devices, _, _, sixteen, _ = mixed_ref.shape
    eight = sixteen // 2
    t = [mixed_ref[:, n, k].astype(F32).reshape(devices * sixteen, 128) for k in range(3)]
    out = []
    for a, b in unpack(*t):
        block = jnp.concatenate([a, b], 1).reshape(devices, 2, eight, WIDE)
        out += [block[:, o].reshape(devices * eight, WIDE) for o in range(2)]
    return out


def update_kernel(mixed_ref, gate_ref, up_ref, cgain_ref, wf_ref, send_ref):
    devices, quads, _, sixteen, _ = mixed_ref.shape
    cgain = as_column(cgain_ref)

    @pl.loop(0, quads, unroll=3)
    def _(n):
        grads = []
        for k, mixed in enumerate(mixed_rows(mixed_ref, n)):
            i = 4 * n + k
            hat, inverse = norm(mixed)
            gu = (up_ref[i].astype(F32) * gate_ref[i]).astype(BF)
            gmn = nn(wf_ref[...], gu)
            back = norm_back(gmn * cgain, hat, inverse)
            grads.append(back.reshape(devices, 1, sixteen // 2, WIDE))
        packed = [
            jnp.concatenate(grads[2 * o : 2 * o + 2], 1).reshape(devices * sixteen, WIDE)
            for o in range(2)
        ]
        for k, v in enumerate(pack(*packed)):
            send_ref[:, n, k] = v.reshape(devices, sixteen, 128).astype(BF)


def result_kernel(
    mixed_ref, mid_ref, normed_ref, gate_ref, up_ref, cgain_ref, wf_ref,
    out_ref, ggate_ref, wfg_ref, wgg_ref, msum_ref, acc,
):
    _, quads, _, _, _ = mixed_ref.shape
    length = out_ref.shape[1]
    wfg_ref[...] = jnp.zeros_like(wfg_ref)
    wgg_ref[...] = jnp.zeros_like(wgg_ref)
    acc[...] = jnp.zeros_like(acc)
    cgain = as_column(cgain_ref)
    for ref in (mixed_ref, mid_ref, normed_ref, gate_ref, up_ref):
        ref.wait()

    @pl.loop(0, quads)
    def _(n):
        for k, mixed in enumerate(mixed_rows(mixed_ref, n)):
            i = 4 * n + k
            hat, _ = norm(mixed)
            mn = (hat * cgain).astype(BF)
            gate = gate_ref[i]
            update = tn(wf_ref[...], mn)
            new = mid_ref[i] + gate * update
            out_ref[i] = new.T[:length].astype(BF)
            upgate = up_ref[i].astype(F32) * gate
            gu = upgate.astype(BF)
            gg = (upgate * update * (1.0 - gate)).astype(BF)
            ggate_ref[i] = gg
            wfg_ref[...] += nt(mn, gu)
            wgg_ref[...] += nt(normed_ref[i], gg)
            acc[...] += nn(wf_ref[...], gu) * hat

    msum_ref[...] = jnp.sum(acc[...].T, 0, keepdims=True)


def edge_back_kernel(
    grads_ref, mid_ref, normed_ref, ggate_ref, up_ref, sig_ref, slope_ref, gain_ref, entry_ref, wg_ref,
    pgrad_ref, pgradt_ref, send_ref, win_ref, gsum_ref, bsum_ref, gacc, bacc, rows,
):
    devices, pairs, _, sixteen, _ = grads_ref.shape
    count, length, channels = pgrad_ref.shape
    win_ref[...] = jnp.zeros_like(win_ref)
    gacc[...] = jnp.zeros_like(gacc)
    bacc[...] = jnp.zeros_like(bacc)
    gain = as_column(gain_ref)
    entry_ref.wait()

    def step(m):
        t = [grads_ref[:, m, k].astype(F32).reshape(devices * sixteen, 128) for k in range(3)]
        for o, (a, b) in enumerate(unpack(*t)):
            i = 2 * m + o
            grad = jnp.concatenate([a, b], 1)
            normed = normed_ref[i]
            slope, sig = slope_ref[i].astype(F32), sig_ref[i].astype(F32)
            graw = jnp.concatenate([grad * slope, grad * sig], 0).astype(BF)
            win_ref[...] += nt(graw, normed)
            gpn = nn(entry_ref[...], graw) + nn(wg_ref[...], ggate_ref[i])
            hat, inverse = norm(mid_ref[i])
            gacc[...] += gpn * hat
            gmid = up_ref[i].astype(F32) + norm_back(gpn * gain, hat, inverse)
            bacc[...] += gmid
            pgradt_ref[i] = gmid.astype(BF)
            turned = gmid.T[:length]
            pgrad_ref[i] = turned.astype(BF)
            rows[pl.ds(i, length, stride=count), :] = turned

    parts = 2
    many = pairs // parts
    for h in range(parts):
        for ref in (mid_ref, normed_ref, ggate_ref, up_ref, sig_ref, slope_ref):
            ref.wait(h)
        pl.loop(h * many, (h + 1) * many, unroll=many)(step)

    send_ref[...] = rows[...].astype(BF)
    gsum_ref[...] = jnp.sum(gacc[...].T, 0, keepdims=True)
    bsum_ref[...] = jnp.sum(bacc[...].T, 0, keepdims=True)


def prepare_kernel(par_ref, own_ref, other_ref, x_ref, left_ref, hat_ref, inv_ref, head, tail):
    chips, pairs, _, half, _ = own_ref.shape
    length = left_ref.shape[1] * 3 // 4
    devices = 2 * chips
    pitch = half + 1
    par = par_ref[0]
    for source, p in ((own_ref, par), (other_ref, 1 - par)):

        @pl.loop(0, chips)
        def _(chip):
            spread_projections(source.at[chip], 2 * chip + p, devices, pitch, head, tail)

    @pl.loop(0, half, unroll=2)
    def _(q):
        left_ref[q] = pad_rows(load_wide(head, tail, q, length, pitch), WIDE).astype(BF)

    width = hat_ref.shape[1]

    @pl.loop(0, pairs)
    def _(m):
        x = flip(x_ref[m].astype(F32))
        for o in range(2):
            hat, inverse = norm(x[o * width : (o + 1) * width])
            hat_ref[2 * m + o] = hat
            inv_ref[2 * m + o] = inverse


def put(stage, i, g):
    half = g.shape[0] // (stage.shape[0] * (stage.shape[2] // WIDE))
    group = stage.shape[2] // WIDE
    at = pl.ds(pl.multiple_of(i * half, half), half)
    for q in range(g.shape[0] // half):
        lanes = slice((q % group) * WIDE, (q % group + 1) * WIDE)
        stage[q // group, at, lanes] = g[q * half : (q + 1) * half]


def contract(stage, projections, total):
    group = stage.shape[2] // WIDE
    total[...] = jnp.zeros_like(total)

    @pl.loop(0, stage.shape[0], unroll=4)
    def _(k):
        r = projections[pl.ds(k * group, group)].reshape(group * WIDE, WIDE)
        total[...] += nn(stage[k], r)


def row_kernel(
    pgradt_ref, right_ref, w_ref, outer_ref, win_ref, wgg_ref, wfg_ref, cgain_ref, pgain_ref,
    bias_ref, grad_ref, out_ref, stage, wacc, wout,
):
    count = pgradt_ref.shape[0]
    many = wacc.shape[0]
    half = right_ref.shape[0]
    depth = 1.0 / (right_ref.shape[1] * 3 // 4)

    @pl.loop(0, count, unroll=4)
    def _(i):
        put(stage, i, nn(w_ref[...], pgradt_ref[i]).astype(BF))

    right_ref.wait()
    contract(stage, right_ref, grad_ref)
    grad_ref[...] = grad_ref[...] * depth
    wacc[...] = jnp.zeros_like(wacc)

    def step(m):
        a = jnp.concatenate([outer_ref[2 * m], outer_ref[2 * m + 1]], 1)
        b = jnp.concatenate([pgradt_ref[2 * m], pgradt_ref[2 * m + 1]], 1)
        wacc[...] += nt(a, b)

    outer_ref.wait()
    pl.loop(0, count // 2, unroll=3)(step)

    for q in range(half):
        wout[pl.ds(q, half, stride=half + 1), :] = wacc[q * half : (q + 1) * half, :]
    for p in range(half):
        out_ref[p * half : (p + 1) * half, :] = wout[
            p * (half + 1) : p * (half + 1) + half, :
        ].astype(BF)
    at = many
    for ref in (win_ref, wgg_ref, wfg_ref):
        out_ref[at : at + ref.shape[0], :] = ref[...].astype(BF)
        at += ref.shape[0]
    rest = [cgain_ref[...], pgain_ref[...], bias_ref[...], jnp.zeros((13, 128), F32)]
    out_ref[at : at + 16, :] = jnp.concatenate(rest, 0).astype(BF)
    at += 16
    out_ref[at:, :] = jnp.zeros((out_ref.shape[0] - at, 128), BF)


def column_kernel(
    pcol_ref, left_ref, w_ref, gleft_ref, hat_ref, inv_ref, mgain_ref, wmap_ref,
    out_ref, cross_ref, prow, stage, gright, cacc,
):
    devices, many, channels = pcol_ref.shape
    half = left_ref.shape[0]
    count = gleft_ref.shape[0] // half
    length = devices * count
    pairs = count // 2

    @pl.loop(0, devices, unroll=4)
    def _(d):
        prow[pl.ds(d * (many + 1), many), :] = pcol_ref[d].astype(F32)

    @pl.loop(0, count, unroll=4)
    def _(j):
        p = jnp.concatenate(
            [prow[pl.ds(j * count + i, devices, stride=many + 1), :] for i in range(count)], 0
        )
        put(stage, j, nt(w_ref[...], pad_rows(p, WIDE).astype(BF)).astype(BF))

    left_ref.wait()
    contract(stage, left_ref, gright)
    gleft_ref.wait()
    hat_ref.wait()
    gain = as_column(mgain_ref)
    cacc[...] = jnp.zeros_like(cacc)

    @pl.loop(0, pairs, unroll=3)
    def _(m):
        both = []
        for o in range(2):
            i = 2 * m + o
            hat = hat_ref[i]
            at = pl.ds(pl.multiple_of(i * half, half), half)
            right = (gright[at, :] * (1.0 / length)).astype(BF)
            g = jnp.concatenate([gleft_ref[at, :].astype(BF), right], 0)
            cacc[...] += nt(hat.astype(BF), pad_rows(g, 128))
            both.append(norm_back(nn(wmap_ref[...], g) * gain, hat, inv_ref[i]))
        out_ref[m] = jnp.concatenate(both, 0).T[:length].astype(BF)

    rows = cross_ref.shape[0]
    cross_ref[...] = (cacc[:rows, :] + pltpu.roll(cacc[rows:, :], 64, 1)).astype(BF)


def finish_kernel(
    factor, all_ref, gain_ref, wmap_ref,
    mgain_out, proj_out, wout_out, bias_out, pgain_out, win_out, wgg_out, cgain_out, wfg_out,
    rows, flat,
):
    everyone, each, _ = all_ref.shape
    width = proj_out.shape[0]
    own = each - width // 2
    eight = 8

    @pl.loop(0, everyone)
    def _(d):
        rows[pl.ds(pl.multiple_of(d * own, 16), own), :] = all_ref[d, :own].astype(F32) * factor

    many = wout_out.shape[0]
    wout_out[...] = rows[:many, :]
    at = many
    channels = wgg_out.shape[0]
    devices = channels // eight
    for k in range(4):
        lr, gv = k // 2, k % 2
        for d in range(devices):
            start = at + gv * 2 * channels + d * 2 * eight + lr * eight
            flat[d * eight : (d + 1) * eight, :] = rows[start : start + eight, :]
        win_out[:, k * channels : (k + 1) * channels] = flat[...].T
    at += 4 * channels
    wgg_out[...] = rows[at : at + channels, :]
    at += channels
    wfg_out[...] = rows[at : at + channels, :]
    at += channels
    cgain_out[...] = rows[at : at + 1, :]
    pgain_out[...] = rows[at + 1 : at + 2, :]
    bias_out[...] = rows[at + 2 : at + 3, :]
    cross = jnp.sum(all_ref[:, own:].astype(F32), 0) * factor
    cross = jnp.concatenate([cross, pltpu.roll(cross, 64, 1)], 0)[:, :width]
    proj_out[...] = cross * as_column(gain_ref)
    mgain_out[...] = as_row(jnp.sum(cross * wmap_ref[...].astype(F32), 1, keepdims=True))


def exchange(v, axes="dap", groups=None):
    return lax.all_to_all(
        v, axes, split_axis=0, concat_axis=0, tiled=True, axis_index_groups=groups
    )


def local(
    homolog_features,
    edge_features,
    adjoint_edges,
    homolog_scaling_factor,
    tensor_mapping_matrix,
    tensor_final_matrix,
    tensor_final_offset,
    edge_scaling_factor,
    trilateral_entry_matrix,
    final_sigmoid_matrix,
    central_scaling_factor,
    trilateral_final_matrix,
):
    n = lax.axis_size("dap")
    msa = homolog_features[0]
    depth, count, width = msa.shape
    length = edge_features.shape[2]
    pairs = count // 2
    half = tensor_mapping_matrix.shape[1] // 2
    channels = edge_features.shape[3]
    eight = channels // n
    edges = edge_features[0]
    adjoint = adjoint_edges[0]
    line = lambda v: v.reshape(1, -1)
    msa_gain = line(homolog_scaling_factor)

    x = msa.reshape(depth, pairs, 2 * width).transpose(1, 0, 2)
    chips = n // 2
    left, right_send, left_send = call(
        2,
        project_kernel,
        [((count, half, WIDE), BF)] + [((chips, pairs, 3, half, 128), BF)] * 2,
        [((pairs, 3, half, 128), BF)] * 2,
        x, msa_gain, tensor_mapping_matrix,
        away=2, sems=(2, chips),
    )
    groups = [list(range(0, n, 2)), list(range(1, n, 2))]

    def sibling(v):
        return lax.ppermute(v, "dap", [(i, i ^ 1) for i in range(n)])

    own = exchange(right_send, groups=groups)
    left_send, own = lax.optimization_barrier((left_send, own))
    other = sibling(own)
    left_own = exchange(left_send, groups=groups)
    parity = lax.rem(lax.axis_index("dap"), 2).astype(jnp.int32).reshape(1)

    qp = tensor_final_matrix.reshape(half, half, channels).transpose(1, 0, 2)
    qp = qp.reshape(half * half, channels)
    entry = trilateral_entry_matrix.reshape(channels, 2, 2, n, eight).transpose(0, 2, 3, 1, 4)
    entry = entry.reshape(channels, 4 * channels)
    wide = ((count, channels, WIDE), BF)
    wide32 = ((count, channels, WIDE), F32)
    every = ((half, WIDE, WIDE), BF)
    outers = ((count, half * half, WIDE), BF)
    spare = [((length * (half + 1), 128), F32)] * 2
    sides = ((count, 2 * channels, WIDE), BF)
    edge_send, mid, normed, sig, slope, right, outer = call(
        14,
        outer_kernel,
        [((n, pairs, 3, 2 * eight, 128), BF), wide32, wide, sides, sides, every, outers],
        spare + [every, outers],
        parity, own, other, left, edges, qp.T, line(tensor_final_offset),
        line(edge_scaling_factor), entry.T, smem=1, away=2,
        far={1: (1, 0), 2: (1, 0), 4: (1, 0), 5: (1, 0), 8: (1, 0)},
    )
    edge_send, left_own = lax.optimization_barrier((edge_send, left_own))
    edge_cols = exchange(edge_send)
    left_other = sibling(left_own)
    gate, up = call(3, gate_kernel, [wide32, wide], [], normed, adjoint, final_sigmoid_matrix)
    rooms = [((length * (2 * eight + 1), 128), F32)] * 2
    rooms += [((length * (eight + 1), 128), F32)] * 2
    mixed_send, left_cols, right_cols = call(
        3,
        triangle_kernel,
        [((n, pairs // 2, 3, 2 * eight, 128), BF)] + [((eight, length, WIDE), BF)] * 2,
        rooms + [((eight, length, WIDE), BF)] * 2,
        edge_cols,
        away=2,
    )
    mixed_send, gate, up = lax.optimization_barrier((mixed_send, gate, up))
    mixed = exchange(mixed_send)
    square = ((channels, channels), F32)
    row = ((1, channels), F32)
    (grad_send,) = call(
        2,
        update_kernel,
        [((n, pairs // 2, 3, 2 * eight, 128), BF)],
        [],
        mixed, gate, up, line(central_scaling_factor), trilateral_final_matrix,
    )
    grad_cols = exchange(grad_send)
    pair_out, grad_gate, tri_out, tri_gate, mid_gain = call(
        6,
        result_kernel,
        [(edges.shape, BF), wide, square, square, row],
        [((channels, WIDE), F32)],
        mixed, mid, normed, gate, up, line(central_scaling_factor), trilateral_final_matrix,
        far={i: (1, 0) for i in range(5)},
    )
    (back_send,) = call(
        4,
        triangle_back_kernel,
        [((n, pairs, 3, 2 * eight, 128), BF)],
        rooms,
        grad_cols, left_cols, right_cols,
        far={1: (1, 0), 2: (1, 0)},
    )
    back = exchange(back_send)
    left_own, left_other, back_send = lax.optimization_barrier((left_own, left_other, back_send))
    lefts, hat, inverse = call(
        6,
        prepare_kernel,
        [every, ((count, width, WIDE), F32), ((count, 1, WIDE), F32)],
        spare,
        parity, left_own, left_other, x, smem=1,
    )
    pgrad, pgradt, pgrad_send, tri_in, tri_gain, bias = call(
        9,
        edge_back_kernel,
        [
            (edges.shape, BF), wide, ((length * count, channels), BF),
            ((4 * channels, channels), F32), row, row,
        ],
        [((channels, WIDE), F32)] * 2 + [((length * count, channels), F32)],
        back, mid, normed, grad_gate, up, sig, slope, line(edge_scaling_factor),
        entry, final_sigmoid_matrix,
        far={**{i: (2, 0) for i in range(1, 7)}, 8: (1, 0)},
    )
    pgrad_cols = exchange(pgrad_send.reshape(n, count * count, channels))
    group = 4
    stage = ((half // group, count * half, group * WIDE), BF)
    grads = ((count * half, WIDE), F32)
    cross = ((width // 2, 128), BF)
    full = ((half * half, channels), F32)
    used = half * half + 6 * channels + 3
    each = -(-used // (16 * n)) * 16
    grad_left, weights = call(
        10,
        row_kernel,
        [grads, ((each * n, channels), BF)],
        [stage, full, ((half * (half + 1), channels), F32)],
        pgradt, right, qp, outer, tri_in, tri_gate, tri_out, mid_gain, tri_gain, bias,
        far={1: (1, 0), 3: (1, 0)},
    )
    weights, pgrad_cols = lax.optimization_barrier((weights, pgrad_cols))
    mine = exchange(weights.reshape(n, each, channels))
    sens, cross = call(
        9,
        column_kernel,
        [((pairs, length, 2 * width), BF), cross],
        [((devices_rows(n, count), channels), F32), stage, grads, ((width, 128), F32)],
        pgrad_cols, lefts, tensor_final_matrix, grad_left, hat, inverse,
        msa_gain, tensor_mapping_matrix,
        far={1: (1, 0), 3: (1, 0), 4: (1, 0)},
    )
    sensitivity = sens.transpose(1, 0, 2).reshape(depth, count, width)
    crops = lax.axis_size("dp")
    mine = jnp.concatenate([jnp.sum(mine.astype(F32), 0).astype(BF), cross], 0)
    mine = exchange(jnp.broadcast_to(mine, (crops,) + mine.shape), "dp")
    mine = jnp.sum(mine.astype(F32), 0).astype(BF)
    total = exchange(jnp.broadcast_to(mine, (n,) + mine.shape))
    factor = 1.0 / (crops * length)
    last = call(
        2,
        lambda *refs: finish_kernel(factor, *refs),
        [
            ((1, width), F32), ((width, 2 * half), F32), full, row, row,
            ((channels, 4 * channels), F32), square, row, square,
        ],
        [((n * each, 128), F32), ((channels, 128), F32)],
        total, msa_gain, tensor_mapping_matrix,
    )
    last = [v.reshape(-1) if v.shape[0] == 1 else v for v in last]
    return (pair_out[None], pgrad[None], sensitivity[None], *last)


def devices_rows(devices, count):
    return devices * (count * count + 1)


def solution(mesh):
    placed = (
        P("dp", None, "dap", None),
        P("dp", "dap", None, None),
        P("dp", "dap", None, None),
    ) + (P(),) * 9
    return jax.shard_map(
        local,
        mesh=mesh,
        in_specs=placed,
        out_specs=(
            P("dp", "dap", None, None),
            P("dp", "dap", None, None),
            P("dp", None, "dap", None),
        )
        + (P(),) * 9,
        check_vma=False,
    )
```

```python
import math

import jax
import jax.numpy as jnp
from jax import lax
from jax.experimental import pallas as pl
from jax.experimental.pallas import tpu as pltpu
from jax.sharding import PartitionSpec as P

EPSILON = 1e-05
BF = jnp.bfloat16
F32 = jnp.float32
WIDE = 256


def nn(a, b):
    return lax.dot_general(a, b, (((1,), (0,)), ((), ())), preferred_element_type=F32)


def nt(a, b):
    return lax.dot_general(a, b, (((1,), (1,)), ((), ())), preferred_element_type=F32)


def tn(a, b):
    return lax.dot_general(a, b, (((0,), (0,)), ((), ())), preferred_element_type=F32)


def norm(v):
    centred = v - jnp.mean(v, 0, keepdims=True)
    inverse = lax.rsqrt(jnp.mean(centred * centred, 0, keepdims=True) + EPSILON)
    return centred * inverse, inverse


def norm_back(h, hat, inverse):
    first = jnp.mean(h, 0, keepdims=True)
    second = jnp.mean(h * hat, 0, keepdims=True)
    return (h - first - hat * second) * inverse


def sigmoid(v):
    return 1.0 / (1.0 + jnp.exp(-v))


def pad_rows(v, rows):
    return jnp.concatenate([v, jnp.zeros((rows - v.shape[0],) + v.shape[1:], v.dtype)], 0)


def flip(v):
    return pad_rows(v, WIDE).T


def low_half(v):
    lane = lax.broadcasted_iota(jnp.int32, v.shape, v.ndim - 1)
    return jnp.where(lane < 64, v, 0.0)


def pack(a, b):
    tail = low_half(a[:, 128:]) + pltpu.roll(low_half(b[:, 128:]), 64, 1)
    return a[:, :128], b[:, :128], tail


def unpack(t0, t1, t2):
    return (t0, low_half(t2)), (t1, low_half(pltpu.roll(t2, 64, 1)))


def as_column(row_ref):
    n = row_ref.shape[1]
    a = lax.broadcasted_iota(jnp.int32, (n, n), 0)
    b = lax.broadcasted_iota(jnp.int32, (n, n), 1)
    return jnp.sum(jnp.where(a == b, row_ref[...], 0.0), 1, keepdims=True)


def as_row(column):
    n = column.shape[0]
    a = lax.broadcasted_iota(jnp.int32, (n, n), 0)
    b = lax.broadcasted_iota(jnp.int32, (n, n), 1)
    return jnp.sum(jnp.where(a == b, column, 0.0), 0, keepdims=True)


class Coming:
    def __init__(self, far, buffer, sems, axis):
        self.far, self.buffer, self.sems, self.axis = far, buffer, sems, axis
        self.shape, self.at = buffer.shape, buffer.at

    def __getitem__(self, index):
        return self.buffer[index]

    def copy(self, k):
        size = self.shape[self.axis] // self.sems.shape[0]
        cut = (slice(None),) * self.axis + (pl.ds(k * size, size),)
        return pltpu.make_async_copy(self.far.at[cut], self.buffer.at[cut], self.sems.at[k])

    def wait(self, k=0):
        self.copy(k).wait()


def call(us, kernel, outs, scratch, *operands, smem=0, away=0, sems=None, far=None):
    far = far or {}
    operands = [
        pltpu.with_memory_space_constraint(v, pltpu.HBM) if i in far else v
        for i, v in enumerate(operands)
    ]
    specs = [pl.BlockSpec(memory_space=pltpu.SMEM)] * smem
    specs += [
        pl.BlockSpec(memory_space=pltpu.HBM if i in far else pltpu.VMEM)
        for i in range(smem, len(operands))
    ]
    room = [pltpu.VMEM(s, t) for s, t in scratch]
    if away:
        room.append(pltpu.SemaphoreType.DMA(sems or (away,)))
    plain = len(operands) + len(outs) + len(room)
    for i, (pieces, _) in far.items():
        room.append(pltpu.VMEM(operands[i].shape, operands[i].dtype))
        room.append(pltpu.SemaphoreType.DMA((pieces,)))

    def wrapped(*refs):
        refs = list(refs)
        for k, (i, (_, axis)) in enumerate(far.items()):
            refs[i] = Coming(refs[i], refs[plain + 2 * k], refs[plain + 2 * k + 1], axis)
        for k in range(max([pieces for pieces, _ in far.values()], default=0)):
            for i, (pieces, _) in far.items():
                if k < pieces:
                    refs[i].copy(k).start()
        kernel(*refs[:plain])

    return pl.pallas_call(
        wrapped,
        out_shape=[
            pltpu.HBM(s, t) if math.prod(s) > 131072 else jax.ShapeDtypeStruct(s, t)
            for s, t in outs
        ],
        in_specs=specs,
        out_specs=[pl.BlockSpec(memory_space=pltpu.VMEM)] * (len(outs) - away)
        + [pl.BlockSpec(memory_space=pltpu.HBM)] * away,
        scratch_shapes=room,
        compiler_params=pltpu.CompilerParams(vmem_limit_bytes=50 * 1024 * 1024),
        cost_estimate=pl.CostEstimate(flops=us * 10**9, bytes_accessed=0, transcendentals=0),
    )(*operands)


def project_kernel(
    x_ref, gain_ref, w_ref, left_ref, rsend_out, lsend_out, rsend_ref, lsend_ref, sems
):
    pairs = x_ref.shape[0]
    width = w_ref.shape[0]
    half = w_ref.shape[1] // 2
    gain = as_column(gain_ref)

    @pl.loop(0, pairs, unroll=3)
    def _(m):
        x = flip(x_ref[m].astype(F32))
        both = []
        for o in range(2):
            hat, _ = norm(x[o * width : (o + 1) * width])
            proj = tn(w_ref[...], (hat * gain).astype(BF))
            both.append(proj)
            left_ref[2 * m + o] = proj[:half].astype(BF)
        for t, v in enumerate(pack(both[0][:half], both[1][:half])):
            lsend_ref[m, t] = v.astype(BF)
        for t, v in enumerate(pack(both[0][half:], both[1][half:])):
            rsend_ref[m, t] = v.astype(BF)

    copies = []
    for k in range(rsend_out.shape[0]):
        copies.append(pltpu.make_async_copy(rsend_ref, rsend_out.at[k], sems.at[0, k]))
        copies.append(pltpu.make_async_copy(lsend_ref, lsend_out.at[k], sems.at[1, k]))
    for c in copies:
        c.start()
    for c in copies:
        c.wait()


def load_wide(head, tail, start, count, stride):
    a = head[pl.ds(start, count, stride=stride), :]
    b = tail[pl.ds(start, count, stride=stride), :]
    return jnp.concatenate([a, b], 1)


def store_wide(head, tail, start, count, stride, v):
    head[pl.ds(start, count, stride=stride), :] = v[:, :128]
    tail[pl.ds(start, count, stride=stride), :] = v[:, 128:]


def spread_projections(source, first, step, pitch, head, tail):
    pairs, _, half, _ = source.shape
    for m in range(pairs):
        t = source[m].astype(F32)
        for o, (a, b) in enumerate(unpack(t[0], t[1], t[2])):
            at = pl.ds((first + step * (2 * m + o)) * pitch, half)
            head[at, :] = a
            tail[at, :] = b


def outer_kernel(
    par_ref, own_ref, other_ref, left_ref, edge_ref, w_ref, bias_ref, gain_ref, entry_ref,
    send_ref, mid_ref, normed_ref, sig_ref, slope_ref, hat_ref, inv_ref, right_out, outer_out,
    head, tail, right_ref, outer_ref, wt_ref, sems,
):
    chips, pairs, _, half, _ = own_ref.shape
    rows = left_ref.shape[0]
    length = edge_ref.shape[1]
    depth = 1.0 / length
    pitch = half + 1
    par = par_ref[0]
    for source, p in ((own_ref, par), (other_ref, 1 - par)):
        source.wait()

        @pl.loop(0, chips, unroll=2)
        def _(chip):
            spread_projections(source.at[chip], (2 * chip + p) * rows, 1, pitch, head, tail)

    left = left_ref[...].reshape(rows * half, WIDE)

    @pl.loop(0, half, unroll=4)
    def _(q):
        r = pad_rows(load_wide(head, tail, q, length, pitch), WIDE).astype(BF)
        right_ref[q] = r
        o = (nt(left, r) * depth).astype(BF)
        at = pl.ds(pl.multiple_of(q * half, half), half)
        for i in range(rows):
            outer_ref[i, at, :] = o[i * half : (i + 1) * half]

    copies = [
        pltpu.make_async_copy(right_ref, right_out, sems.at[0]),
        pltpu.make_async_copy(outer_ref, outer_out, sems.at[1]),
    ]
    for c in copies:
        c.start()
    devices, _, _, sixteen, _ = send_ref.shape
    bias = as_column(bias_ref)
    gain = as_column(gain_ref)
    for ref in (edge_ref, w_ref, entry_ref):
        ref.wait()
    wt_ref[...] = w_ref[...].astype(F32).T.astype(BF)

    @pl.loop(0, pairs, unroll=3)
    def _(m):
        both = []
        for o in range(2):
            i = 2 * m + o
            mid = flip(edge_ref[i].astype(F32)) + (nn(wt_ref[...], outer_ref[i]) + bias)
            mid_ref[i] = mid
            hat, inverse = norm(mid)
            hat_ref[i] = hat
            inv_ref[i] = inverse
            normed = (hat * gain).astype(BF)
            normed_ref[i] = normed
            raw = nn(entry_ref[...], normed)
            cut = raw.shape[0] // 2
            sig = sigmoid(raw[:cut])
            edge = sig * raw[cut:]
            both.append(edge)
            sig_ref[i] = sig.astype(BF)
            slope_ref[i] = (edge * (1.0 - sig)).astype(BF)
        for t, v in enumerate(pack(*both)):
            send_ref[:, m, t] = v.reshape(devices, sixteen, 128).astype(BF)

    for c in copies:
        c.wait()


def gate_kernel(normed_ref, adj_ref, wg_ref, gate_ref, up_ref):
    @pl.loop(0, normed_ref.shape[0])
    def _(i):
        gate_ref[i] = sigmoid(tn(wg_ref[...], normed_ref[i]))
        up_ref[i] = flip(adj_ref[i].astype(F32)).astype(BF)


def spread(source, half, head, tail):
    devices, pairs, _, high, _ = source.shape
    many = high // half

    @pl.loop(0, devices, unroll=4)
    def _(d):
        for m in range(pairs):
            t = source[d, m].astype(F32)
            for o, (a, b) in enumerate(unpack(t[0], t[1], t[2])):
                for g in range(many):
                    at = pl.ds((((d * pairs + m) * 2 + o) * many + g) * (half + 1), half)
                    head[at, :] = a[g * half : (g + 1) * half]
                    tail[at, :] = b[g * half : (g + 1) * half]


def gather_up(half, head, tail, target):
    devices, pairs, _, high, _ = target.shape
    many = high // half

    @pl.loop(0, devices, unroll=4)
    def _(d):
        for m in range(pairs):
            wide = []
            for o in range(2):
                got = []
                for g in range(many):
                    at = pl.ds((((d * pairs + m) * 2 + o) * many + g) * (half + 1), half)
                    got.append(jnp.concatenate([head[at, :], tail[at, :]], 1))
                wide.append(jnp.concatenate(got, 0))
            for t, v in enumerate(pack(*wide)):
                target[d, m, t] = v.astype(BF)


def triangle_kernel(
    edges_ref, send_ref, left_out, right_out, head, tail, mhead, mtail, left_ref, right_ref, sems
):
    channels, length, _ = left_ref.shape
    spread(edges_ref, 2 * channels, head, tail)
    for c in range(channels):
        a = load_wide(head, tail, c, length, 2 * channels + 1).astype(BF)
        b = load_wide(head, tail, channels + c, length, 2 * channels + 1).astype(BF)
        left_ref[c] = a
        right_ref[c] = b
        mixed = tn(a, b)[:length]
        store_wide(mhead, mtail, c, length, channels + 1, mixed)
    copies = [
        pltpu.make_async_copy(left_ref, left_out, sems.at[0]),
        pltpu.make_async_copy(right_ref, right_out, sems.at[1]),
    ]
    for c in copies:
        c.start()
    gather_up(channels, mhead, mtail, send_ref)
    for c in copies:
        c.wait()


def triangle_back_kernel(grads_ref, left_ref, right_ref, send_ref, head, tail, mhead, mtail):
    channels, length, _ = left_ref.shape
    spread(grads_ref, channels, mhead, mtail)
    left_ref.wait()
    right_ref.wait()
    for c in range(channels):
        g = pad_rows(load_wide(mhead, mtail, c, length, channels + 1), WIDE).astype(BF)
        store_wide(head, tail, c, length, 2 * channels + 1, nt(right_ref[c], g))
        store_wide(head, tail, channels + c, length, 2 * channels + 1, nn(left_ref[c], g))
    gather_up(2 * channels, head, tail, send_ref)


def mixed_rows(mixed_ref, n):
    devices, _, _, sixteen, _ = mixed_ref.shape
    eight = sixteen // 2
    t = [mixed_ref[:, n, k].astype(F32).reshape(devices * sixteen, 128) for k in range(3)]
    out = []
    for a, b in unpack(*t):
        block = jnp.concatenate([a, b], 1).reshape(devices, 2, eight, WIDE)
        out += [block[:, o].reshape(devices * eight, WIDE) for o in range(2)]
    return out


def update_kernel(mixed_ref, gate_ref, up_ref, cgain_ref, wf_ref, send_ref):
    devices, quads, _, sixteen, _ = mixed_ref.shape
    cgain = as_column(cgain_ref)

    @pl.loop(0, quads, unroll=3)
    def _(n):
        grads = []
        for k, mixed in enumerate(mixed_rows(mixed_ref, n)):
            i = 4 * n + k
            hat, inverse = norm(mixed)
            gu = (up_ref[i].astype(F32) * gate_ref[i]).astype(BF)
            gmn = nn(wf_ref[...], gu)
            back = norm_back(gmn * cgain, hat, inverse)
            grads.append(back.reshape(devices, 1, sixteen // 2, WIDE))
        packed = [
            jnp.concatenate(grads[2 * o : 2 * o + 2], 1).reshape(devices * sixteen, WIDE)
            for o in range(2)
        ]
        for k, v in enumerate(pack(*packed)):
            send_ref[:, n, k] = v.reshape(devices, sixteen, 128).astype(BF)


def result_kernel(
    mixed_ref, mid_ref, normed_ref, gate_ref, up_ref, cgain_ref, wf_ref,
    out_ref, ggate_ref, wfg_ref, wgg_ref, msum_ref, acc,
):
    _, quads, _, _, _ = mixed_ref.shape
    length = out_ref.shape[1]
    wfg_ref[...] = jnp.zeros_like(wfg_ref)
    wgg_ref[...] = jnp.zeros_like(wgg_ref)
    acc[...] = jnp.zeros_like(acc)
    cgain = as_column(cgain_ref)
    for ref in (mixed_ref, mid_ref, normed_ref, gate_ref, up_ref):
        ref.wait()

    @pl.loop(0, quads)
    def _(n):
        for k, mixed in enumerate(mixed_rows(mixed_ref, n)):
            i = 4 * n + k
            hat, _ = norm(mixed)
            mn = (hat * cgain).astype(BF)
            gate = gate_ref[i]
            update = tn(wf_ref[...], mn)
            new = mid_ref[i] + gate * update
            out_ref[i] = new.T[:length].astype(BF)
            upgate = up_ref[i].astype(F32) * gate
            gu = upgate.astype(BF)
            gg = (upgate * update * (1.0 - gate)).astype(BF)
            ggate_ref[i] = gg
            wfg_ref[...] += nt(mn, gu)
            wgg_ref[...] += nt(normed_ref[i], gg)
            acc[...] += nn(wf_ref[...], gu) * hat

    msum_ref[...] = jnp.sum(acc[...].T, 0, keepdims=True)


def edge_back_kernel(
    grads_ref, hat_ref, normed_ref, ggate_ref, up_ref, sig_ref, slope_ref, gain_ref, entry_ref, wg_ref, inv_ref,
    pgrad_ref, pgradt_ref, send_ref, win_ref, gsum_ref, bsum_ref, gacc, bacc, rows,
):
    devices, pairs, _, sixteen, _ = grads_ref.shape
    count, length, channels = pgrad_ref.shape
    win_ref[...] = jnp.zeros_like(win_ref)
    gacc[...] = jnp.zeros_like(gacc)
    bacc[...] = jnp.zeros_like(bacc)
    gain = as_column(gain_ref)
    entry_ref.wait()

    def step(m):
        t = [grads_ref[:, m, k].astype(F32).reshape(devices * sixteen, 128) for k in range(3)]
        for o, (a, b) in enumerate(unpack(*t)):
            i = 2 * m + o
            grad = jnp.concatenate([a, b], 1)
            normed = normed_ref[i]
            slope, sig = slope_ref[i].astype(F32), sig_ref[i].astype(F32)
            graw = jnp.concatenate([grad * slope, grad * sig], 0).astype(BF)
            win_ref[...] += nt(graw, normed)
            gpn = nn(entry_ref[...], graw) + nn(wg_ref[...], ggate_ref[i])
            hat, inverse = hat_ref[i], inv_ref[i]
            gacc[...] += gpn * hat
            gmid = up_ref[i].astype(F32) + norm_back(gpn * gain, hat, inverse)
            bacc[...] += gmid
            pgradt_ref[i] = gmid.astype(BF)
            turned = gmid.T[:length]
            pgrad_ref[i] = turned.astype(BF)
            rows[pl.ds(i, length, stride=count), :] = turned

    parts = 2
    many = pairs // parts
    for h in range(parts):
        for ref in (hat_ref, normed_ref, ggate_ref, up_ref, sig_ref, slope_ref):
            ref.wait(h)
        pl.loop(h * many, (h + 1) * many, unroll=many)(step)

    send_ref[...] = rows[...].astype(BF)
    gsum_ref[...] = jnp.sum(gacc[...].T, 0, keepdims=True)
    bsum_ref[...] = jnp.sum(bacc[...].T, 0, keepdims=True)


def prepare_kernel(par_ref, own_ref, other_ref, x_ref, left_ref, hat_ref, inv_ref, head, tail):
    chips, pairs, _, half, _ = own_ref.shape
    length = left_ref.shape[1] * 3 // 4
    devices = 2 * chips
    pitch = half + 1
    par = par_ref[0]
    for source, p in ((own_ref, par), (other_ref, 1 - par)):

        @pl.loop(0, chips)
        def _(chip):
            spread_projections(source.at[chip], 2 * chip + p, devices, pitch, head, tail)

    @pl.loop(0, half, unroll=2)
    def _(q):
        left_ref[q] = pad_rows(load_wide(head, tail, q, length, pitch), WIDE).astype(BF)

    width = hat_ref.shape[1]

    @pl.loop(0, pairs)
    def _(m):
        x = flip(x_ref[m].astype(F32))
        for o in range(2):
            hat, inverse = norm(x[o * width : (o + 1) * width])
            hat_ref[2 * m + o] = hat
            inv_ref[2 * m + o] = inverse


def put(stage, i, g):
    half = g.shape[0] // (stage.shape[0] * (stage.shape[2] // WIDE))
    group = stage.shape[2] // WIDE
    at = pl.ds(pl.multiple_of(i * half, half), half)
    for q in range(g.shape[0] // half):
        lanes = slice((q % group) * WIDE, (q % group + 1) * WIDE)
        stage[q // group, at, lanes] = g[q * half : (q + 1) * half]


def contract(stage, projections, total):
    group = stage.shape[2] // WIDE
    total[...] = jnp.zeros_like(total)

    @pl.loop(0, stage.shape[0], unroll=4)
    def _(k):
        r = projections[pl.ds(k * group, group)].reshape(group * WIDE, WIDE)
        total[...] += nn(stage[k], r)


def row_kernel(
    pgradt_ref, right_ref, w_ref, outer_ref, win_ref, wgg_ref, wfg_ref, cgain_ref, pgain_ref,
    bias_ref, grad_ref, out_ref, stage, wacc, wout,
):
    count = pgradt_ref.shape[0]
    many = wacc.shape[0]
    half = right_ref.shape[0]
    depth = 1.0 / (right_ref.shape[1] * 3 // 4)

    @pl.loop(0, count, unroll=4)
    def _(i):
        put(stage, i, nn(w_ref[...], pgradt_ref[i]).astype(BF))

    right_ref.wait()
    contract(stage, right_ref, grad_ref)
    grad_ref[...] = grad_ref[...] * depth
    wacc[...] = jnp.zeros_like(wacc)

    def step(m):
        a = jnp.concatenate([outer_ref[2 * m], outer_ref[2 * m + 1]], 1)
        b = jnp.concatenate([pgradt_ref[2 * m], pgradt_ref[2 * m + 1]], 1)
        wacc[...] += nt(a, b)

    outer_ref.wait()
    pl.loop(0, count // 2, unroll=3)(step)

    for q in range(half):
        wout[pl.ds(q, half, stride=half + 1), :] = wacc[q * half : (q + 1) * half, :]
    for p in range(half):
        out_ref[p * half : (p + 1) * half, :] = wout[
            p * (half + 1) : p * (half + 1) + half, :
        ].astype(BF)
    at = many
    for ref in (win_ref, wgg_ref, wfg_ref):
        out_ref[at : at + ref.shape[0], :] = ref[...].astype(BF)
        at += ref.shape[0]
    rest = [cgain_ref[...], pgain_ref[...], bias_ref[...], jnp.zeros((13, 128), F32)]
    out_ref[at : at + 16, :] = jnp.concatenate(rest, 0).astype(BF)
    at += 16
    out_ref[at:, :] = jnp.zeros((out_ref.shape[0] - at, 128), BF)


def column_kernel(
    pcol_ref, left_ref, w_ref, gleft_ref, hat_ref, inv_ref, mgain_ref, wmap_ref,
    out_ref, cross_ref, prow, stage, gright, cacc,
):
    devices, many, channels = pcol_ref.shape
    half = left_ref.shape[0]
    count = gleft_ref.shape[0] // half
    length = devices * count
    pairs = count // 2

    @pl.loop(0, devices, unroll=4)
    def _(d):
        prow[pl.ds(d * (many + 1), many), :] = pcol_ref[d].astype(F32)

    @pl.loop(0, count, unroll=4)
    def _(j):
        p = jnp.concatenate(
            [prow[pl.ds(j * count + i, devices, stride=many + 1), :] for i in range(count)], 0
        )
        put(stage, j, nt(w_ref[...], pad_rows(p, WIDE).astype(BF)).astype(BF))

    left_ref.wait()
    contract(stage, left_ref, gright)
    gleft_ref.wait()
    hat_ref.wait()
    gain = as_column(mgain_ref)
    cacc[...] = jnp.zeros_like(cacc)

    @pl.loop(0, pairs, unroll=3)
    def _(m):
        both = []
        for o in range(2):
            i = 2 * m + o
            hat = hat_ref[i]
            at = pl.ds(pl.multiple_of(i * half, half), half)
            right = (gright[at, :] * (1.0 / length)).astype(BF)
            g = jnp.concatenate([gleft_ref[at, :].astype(BF), right], 0)
            cacc[...] += nt(hat.astype(BF), pad_rows(g, 128))
            both.append(norm_back(nn(wmap_ref[...], g) * gain, hat, inv_ref[i]))
        out_ref[m] = jnp.concatenate(both, 0).T[:length].astype(BF)

    rows = cross_ref.shape[0]
    cross_ref[...] = (cacc[:rows, :] + pltpu.roll(cacc[rows:, :], 64, 1)).astype(BF)


def finish_kernel(
    factor, all_ref, gain_ref, wmap_ref,
    mgain_out, proj_out, wout_out, bias_out, pgain_out, win_out, wgg_out, cgain_out, wfg_out,
    rows, flat,
):
    everyone, each, _ = all_ref.shape
    width = proj_out.shape[0]
    own = each - width // 2
    eight = 8

    @pl.loop(0, everyone)
    def _(d):
        rows[pl.ds(pl.multiple_of(d * own, 16), own), :] = all_ref[d, :own].astype(F32) * factor

    many = wout_out.shape[0]
    wout_out[...] = rows[:many, :]
    at = many
    channels = wgg_out.shape[0]
    devices = channels // eight
    for k in range(4):
        lr, gv = k // 2, k % 2
        for d in range(devices):
            start = at + gv * 2 * channels + d * 2 * eight + lr * eight
            flat[d * eight : (d + 1) * eight, :] = rows[start : start + eight, :]
        win_out[:, k * channels : (k + 1) * channels] = flat[...].T
    at += 4 * channels
    wgg_out[...] = rows[at : at + channels, :]
    at += channels
    wfg_out[...] = rows[at : at + channels, :]
    at += channels
    cgain_out[...] = rows[at : at + 1, :]
    pgain_out[...] = rows[at + 1 : at + 2, :]
    bias_out[...] = rows[at + 2 : at + 3, :]
    cross = jnp.sum(all_ref[:, own:].astype(F32), 0) * factor
    cross = jnp.concatenate([cross, pltpu.roll(cross, 64, 1)], 0)[:, :width]
    proj_out[...] = cross * as_column(gain_ref)
    mgain_out[...] = as_row(jnp.sum(cross * wmap_ref[...].astype(F32), 1, keepdims=True))


def exchange(v, axes="dap", groups=None):
    return lax.all_to_all(
        v, axes, split_axis=0, concat_axis=0, tiled=True, axis_index_groups=groups
    )


def local(
    homolog_features,
    edge_features,
    adjoint_edges,
    homolog_scaling_factor,
    tensor_mapping_matrix,
    tensor_final_matrix,
    tensor_final_offset,
    edge_scaling_factor,
    trilateral_entry_matrix,
    final_sigmoid_matrix,
    central_scaling_factor,
    trilateral_final_matrix,
):
    n = lax.axis_size("dap")
    msa = homolog_features[0]
    depth, count, width = msa.shape
    length = edge_features.shape[2]
    pairs = count // 2
    half = tensor_mapping_matrix.shape[1] // 2
    channels = edge_features.shape[3]
    eight = channels // n
    edges = edge_features[0]
    adjoint = adjoint_edges[0]
    line = lambda v: v.reshape(1, -1)
    msa_gain = line(homolog_scaling_factor)

    x = msa.reshape(depth, pairs, 2 * width).transpose(1, 0, 2)
    chips = n // 2
    left, right_send, left_send = call(
        2,
        project_kernel,
        [((count, half, WIDE), BF)] + [((chips, pairs, 3, half, 128), BF)] * 2,
        [((pairs, 3, half, 128), BF)] * 2,
        x, msa_gain, tensor_mapping_matrix,
        away=2, sems=(2, chips),
    )
    groups = [list(range(0, n, 2)), list(range(1, n, 2))]

    def sibling(v):
        return lax.ppermute(v, "dap", [(i, i ^ 1) for i in range(n)])

    own = exchange(right_send, groups=groups)
    left_send, own = lax.optimization_barrier((left_send, own))
    other = sibling(own)
    left_own = exchange(left_send, groups=groups)
    parity = lax.rem(lax.axis_index("dap"), 2).astype(jnp.int32).reshape(1)

    qp = tensor_final_matrix.reshape(half, half, channels).transpose(1, 0, 2)
    qp = qp.reshape(half * half, channels)
    entry = trilateral_entry_matrix.reshape(channels, 2, 2, n, eight).transpose(0, 2, 3, 1, 4)
    entry = entry.reshape(channels, 4 * channels)
    wide = ((count, channels, WIDE), BF)
    wide32 = ((count, channels, WIDE), F32)
    every = ((half, WIDE, WIDE), BF)
    outers = ((count, half * half, WIDE), BF)
    spare = [((length * (half + 1), 128), F32)] * 2
    sides = ((count, 2 * channels, WIDE), BF)
    edge_send, mid, normed, sig, slope, pair_hat, pair_inv, right, outer = call(
        14,
        outer_kernel,
        [((n, pairs, 3, 2 * eight, 128), BF), wide32, wide, sides, sides, wide32, ((count, 1, WIDE), F32), every, outers],
        spare + [every, outers, ((channels, half * half), BF)],
        parity, own, other, left, edges, qp, line(tensor_final_offset),
        line(edge_scaling_factor), entry.T, smem=1, away=2,
        far={1: (1, 0), 2: (1, 0), 4: (1, 0), 5: (1, 0), 8: (1, 0)},
    )
    edge_send, left_own = lax.optimization_barrier((edge_send, left_own))
    edge_cols = exchange(edge_send)
    left_other = sibling(left_own)
    gate, up = call(3, gate_kernel, [wide32, wide], [], normed, adjoint, final_sigmoid_matrix)
    rooms = [((length * (2 * eight + 1), 128), F32)] * 2
    rooms += [((length * (eight + 1), 128), F32)] * 2
    mixed_send, left_cols, right_cols = call(
        3,
        triangle_kernel,
        [((n, pairs // 2, 3, 2 * eight, 128), BF)] + [((eight, length, WIDE), BF)] * 2,
        rooms + [((eight, length, WIDE), BF)] * 2,
        edge_cols,
        away=2,
    )
    mixed_send, gate, up = lax.optimization_barrier((mixed_send, gate, up))
    mixed = exchange(mixed_send)
    square = ((channels, channels), F32)
    row = ((1, channels), F32)
    (grad_send,) = call(
        2,
        update_kernel,
        [((n, pairs // 2, 3, 2 * eight, 128), BF)],
        [],
        mixed, gate, up, line(central_scaling_factor), trilateral_final_matrix,
    )
    grad_cols = exchange(grad_send)
    pair_out, grad_gate, tri_out, tri_gate, mid_gain = call(
        6,
        result_kernel,
        [(edges.shape, BF), wide, square, square, row],
        [((channels, WIDE), F32)],
        mixed, mid, normed, gate, up, line(central_scaling_factor), trilateral_final_matrix,
        far={i: (1, 0) for i in range(5)},
    )
    (back_send,) = call(
        4,
        triangle_back_kernel,
        [((n, pairs, 3, 2 * eight, 128), BF)],
        rooms,
        grad_cols, left_cols, right_cols,
        far={1: (1, 0), 2: (1, 0)},
    )
    back = exchange(back_send)
    left_own, left_other, back_send = lax.optimization_barrier((left_own, left_other, back_send))
    lefts, hat, inverse = call(
        6,
        prepare_kernel,
        [every, ((count, width, WIDE), F32), ((count, 1, WIDE), F32)],
        spare,
        parity, left_own, left_other, x, smem=1,
    )
    pgrad, pgradt, pgrad_send, tri_in, tri_gain, bias = call(
        9,
        edge_back_kernel,
        [
            (edges.shape, BF), wide, ((length * count, channels), BF),
            ((4 * channels, channels), F32), row, row,
        ],
        [((channels, WIDE), F32)] * 2 + [((length * count, channels), F32)],
        back, pair_hat, normed, grad_gate, up, sig, slope, line(edge_scaling_factor),
        entry, final_sigmoid_matrix, pair_inv,
        far={**{i: (2, 0) for i in range(1, 7)}, 8: (1, 0)},
    )
    pgrad_cols = exchange(pgrad_send.reshape(n, count * count, channels))
    group = 4
    stage = ((half // group, count * half, group * WIDE), BF)
    grads = ((count * half, WIDE), F32)
    cross = ((width // 2, 128), BF)
    full = ((half * half, channels), F32)
    used = half * half + 6 * channels + 3
    each = -(-used // (16 * n)) * 16
    grad_left, weights = call(
        10,
        row_kernel,
        [grads, ((each * n, channels), BF)],
        [stage, full, ((half * (half + 1), channels), F32)],
        pgradt, right, qp, outer, tri_in, tri_gate, tri_out, mid_gain, tri_gain, bias,
        far={1: (1, 0), 3: (1, 0)},
    )
    weights, pgrad_cols = lax.optimization_barrier((weights, pgrad_cols))
    mine = exchange(weights.reshape(n, each, channels))
    sens, cross = call(
        9,
        column_kernel,
        [((pairs, length, 2 * width), BF), cross],
        [((devices_rows(n, count), channels), F32), stage, grads, ((width, 128), F32)],
        pgrad_cols, lefts, tensor_final_matrix, grad_left, hat, inverse,
        msa_gain, tensor_mapping_matrix,
        far={1: (1, 0), 3: (1, 0), 4: (1, 0)},
    )
    sensitivity = sens.transpose(1, 0, 2).reshape(depth, count, width)
    crops = lax.axis_size("dp")
    mine = jnp.concatenate([jnp.sum(mine.astype(F32), 0).astype(BF), cross], 0)
    mine = exchange(jnp.broadcast_to(mine, (crops,) + mine.shape), "dp")
    mine = jnp.sum(mine.astype(F32), 0).astype(BF)
    total = exchange(jnp.broadcast_to(mine, (n,) + mine.shape))
    factor = 1.0 / (crops * length)
    last = call(
        2,
        lambda *refs: finish_kernel(factor, *refs),
        [
            ((1, width), F32), ((width, 2 * half), F32), full, row, row,
            ((channels, 4 * channels), F32), square, row, square,
        ],
        [((n * each, 128), F32), ((channels, 128), F32)],
        total, msa_gain, tensor_mapping_matrix,
    )
    last = [v.reshape(-1) if v.shape[0] == 1 else v for v in last]
    return (pair_out[None], pgrad[None], sensitivity[None], *last)


def devices_rows(devices, count):
    return devices * (count * count + 1)


def solution(mesh):
    placed = (
        P("dp", None, "dap", None),
        P("dp", "dap", None, None),
        P("dp", "dap", None, None),
    ) + (P(),) * 9
    return jax.shard_map(
        local,
        mesh=mesh,
        in_specs=placed,
        out_specs=(
            P("dp", "dap", None, None),
            P("dp", "dap", None, None),
            P("dp", None, "dap", None),
        )
        + (P(),) * 9,
        check_vma=False,
    )
```
